512 devices in a mesh: gz: 16 (over y, core), xy: 32 (over x, z).
Axes of the slice: x: 4, y: 8, z: 8, core: 2. Of those that a mesh axis runs over, the one named last changes fastest.
Arguments:
- design: float32 [128, 512, 1024], P('gz', 'xy'), may hold values from 0 to 1
Outputs:
- blueprint: float32 [128, 512, 1024], P('gz', 'xy')
- printed: float32 [128, 512, 1024], P('gz', 'xy')
The draws below stay inside these ranges and needn't reach their ends.
All inputs are finite; a program needn't handle non-finite values.
Results may differ from the reference program's by a relative error of at most 0.000054.
Values sent between devices are 32-bit elements; how exact they have to be, the bound alone decides.
No kernel may reach another device: no remote copies, remote signals or barrier semaphores. Data moves between devices by JAX's collectives and lax.ppermute only.
A program may use at most 64 MiB of HBM per device.

```python
import math
import jax
import jax.numpy as jnp
from jax import lax

NY = 1024
ITERS = 3
NZ = 128
NX = 512


def shard_levels(stream_key, dims, pieces, smallest, high):
    gain = 1.0
    for axis_at, shards_of in pieces:
        draws = jax.random.uniform(jax.random.fold_in(jax.random.fold_in(stream_key, 6), axis_at), (shards_of,), jnp.float32, smallest / len(pieces), high / len(pieces))
        gain = gain * jnp.repeat(jnp.exp(draws), dims[axis_at] // shards_of).reshape((-1,) + (1,) * (len(dims) - 1 - axis_at))
    return gain


def setup_inputs(seed: int = 0) -> dict:
    key_of = jax.random.split(jax.random.key(seed), 2)
    design = jnp.clip(1.0 * jax.random.uniform(key_of[0], (NZ, NX, NY), jnp.float32) ** shard_levels(key_of[0], (NZ, NX, NY), ((0, 16), (1, 32)), -0.2, 0.2), 0.0, 1.0)
    return {"design": design}


FILTER_R2 = 4.0
PROJ_BETA = 8.0
PROJ_ETA = 0.5
SHARPNESS = 16.0
SMOOTH_EPS = 0.0001

def neighbour_sum(padded):
    beside = padded[2:, 1:-1, 1:-1] + padded[:-2, 1:-1, 1:-1]
    beside = beside + padded[1:-1, 2:, 1:-1] + padded[1:-1, :-2, 1:-1]
    beside = beside + padded[1:-1, 1:-1, 2:] + padded[1:-1, 1:-1, :-2]
    return beside

def project(field):
    upper = jnp.tanh(PROJ_BETA * PROJ_ETA) + jnp.tanh(PROJ_BETA * (field - PROJ_ETA))
    lower = math.tanh(PROJ_BETA * PROJ_ETA) + math.tanh(PROJ_BETA * (1.0 - PROJ_ETA))
    return upper / lower

def smooth_min(first, second):
    gap = first - second
    return 0.5 * (first + second - jnp.sqrt(gap * gap + SMOOTH_EPS) + math.sqrt(SMOOTH_EPS))

def support_of(below_layer):
    weights = jnp.pad(jnp.exp(SHARPNESS * below_layer), 1)
    count_rows = below_layer.shape[0]
    count_cols = below_layer.shape[1]
    total = jnp.zeros(below_layer.shape, jnp.float32)
    for shift_a in range(3):
        for shift_b in range(3):
            total = total + weights[shift_a:shift_a + count_rows, shift_b:shift_b + count_cols]
    return (jnp.log(total) - math.log(9.0)) / SHARPNESS

def reference(design):
    field = design
    for sweep_no in range(ITERS):
        padded = jnp.pad(field, 1)
        field = (design + FILTER_R2 * neighbour_sum(padded)) / (1.0 + 6.0 * FILTER_R2)
    blueprint = project(field)

    def layer_step(below_layer, blue_layer):
        printed_layer = smooth_min(blue_layer, support_of(below_layer))
        return (printed_layer, printed_layer)
    first_below = jnp.ones(blueprint.shape[1:], jnp.float32)
    unused, printed = lax.scan(layer_step, first_below, blueprint)
    return (blueprint, printed)
```

```python
import functools
import math

import jax
import jax.numpy as jnp
from jax import lax
from jax.experimental import pallas as pl
from jax.experimental.pallas import tpu as pltpu
from jax.sharding import PartitionSpec as P

LAYERS = 16
ROWS = 16
FOLDS = 8
LANES = 128
STRIDE = 80
HALO = 24
REACH = 3
PART = 768
AXES = ("gz", "xy")

FILTER_R2 = 4.0
PROJ_BETA = 8.0
PROJ_ETA = 0.5
SHARPNESS = 16.0
SMOOTH_EPS = 0.0001
HALF = 0.5 * SHARPNESS / math.log(2.0)
OUTSIDE = -50.0
TINY = 2.0**-100
MARGIN_AT = [sum(15 - j for j in range(k)) for k in range(16)]
MARGIN = MARGIN_AT[15]
SIDE = 20 + 18 + 16


def place():
    slab = lax.axis_index("gz")
    return lax.div(slab, 2), lax.rem(slab, 2), lax.axis_index("xy")


def lane_of(shape=(FOLDS, LANES)):
    return lax.broadcasted_iota(jnp.int32, shape, len(shape) - 1)


def column_mask(core):
    fold = lax.broadcasted_iota(jnp.int32, (FOLDS, LANES), 0)
    column = 384 * core + STRIDE * fold + lane_of() - HALO
    return (column >= 0) & (column < 1024)


def fold_kernel(own, partner, near, far, out, to_down, to_up):
    unused, core, unused = place()
    lane = lane_of()

    def fold(source, start, base, count):
        def layer(i, carry):
            for group in range(2):
                tiles = []
                for a in range(7):
                    at = jnp.clip(a - 1 + core, 0, 5) * LANES + start
                    tile = source[i, pl.ds(8 * group, 8), pl.ds(pl.multiple_of(at, LANES), LANES)]
                    if a == 0:
                        tile = jnp.where(core == 0, 0.0, tile)
                    if a == 6:
                        tile = jnp.where(core == 1, 0.0, tile)
                    tiles.append(tile)
                for s in range(FOLDS):
                    a, shift = divmod(LANES - HALO + STRIDE * s, LANES)
                    block = tiles[a]
                    if shift:
                        first = pltpu.roll(tiles[a], LANES - shift, 1)
                        second = pltpu.roll(tiles[a + 1], LANES - shift, 1)
                        block = jnp.where(lane < LANES - shift, first, second)
                    row = ((base + i) * ROWS + 8 * group) * FOLDS
                    out[pl.ds(row + s, 8, stride=FOLDS), :] = block
            return carry

        lax.fori_loop(0, count, layer, 0)

    fold(own, 256 * core, REACH + 8 * core, 8)
    fold(partner, 0, REACH + 8 * (1 - core), 8)
    fold(near, 0, 19 * core, REACH)
    fold(far, 0, 19 * (1 - core), REACH)
    at = 0
    for away in range(REACH):
        for i in range(1 + away, 21 - away):
            to_down[at] = out[pl.ds((i * ROWS + 15 - away) * FOLDS, FOLDS), :]
            to_up[at] = out[pl.ds((i * ROWS + away) * FOLDS, FOLDS), :]
            at += 1


def filter_kernel(count_chips, count_tiles, own, up, down, height, to_down, to_up, cells, first, second):
    chip, core, tile = place()
    inside = column_mask(core)
    scale = jnp.where(inside, 1.0 / (1.0 + 6.0 * FILTER_R2), 0.0)
    above = jnp.where(tile > 0, 1.0, 0.0)
    below = jnp.where(tile < count_tiles - 1, 1.0, 0.0)

    def gather(i, carry):
        cells[i, pl.ds(REACH, ROWS)] = own[i]
        return carry

    lax.fori_loop(0, 22, gather, 0)
    at = 0
    for away in range(REACH):
        for i in range(1 + away, 21 - away):
            cells[i, REACH - 1 - away] = up[at]
            cells[i, REACH + ROWS + away] = down[at]
            at += 1

    def sweep(source, step, store):
        rim = REACH - step

        def layer(i, rows):
            held = jnp.where(((chip == 0) & (i < REACH)) | ((chip == count_chips - 1) & (i >= REACH + LAYERS)), 0.0, scale)
            for r in rows:
                middle = source[i, r]
                total = source[i - 1, r] + source[i + 1, r] + source[i, r - 1] + source[i, r + 1]
                total = total + pltpu.roll(middle, 1, 1) + pltpu.roll(middle, LANES - 1, 1)
                factor = held
                if r < REACH:
                    factor = held * above
                if r >= REACH + ROWS:
                    factor = held * below
                store(i, r, (cells[i, r] + FILTER_R2 * total) * factor)

        def body(i, carry):
            layer(i, range(REACH - rim, REACH + ROWS + rim))
            return carry

        for away in range(rim):
            for i in (REACH - rim + away, REACH + LAYERS + rim - 1 - away):
                layer(i, range(REACH - away, REACH + ROWS + away))
        lax.fori_loop(REACH, REACH + LAYERS, body, 0)

    def keep(target):
        def store(i, r, value):
            target[i, r] = value

        return store

    base = math.tanh(PROJ_BETA * PROJ_ETA)
    gain = HALF / (math.tanh(PROJ_BETA * PROJ_ETA) + math.tanh(PROJ_BETA * (1.0 - PROJ_ETA)))

    def project(i, r, field):
        value = gain * (base + jnp.tanh(PROJ_BETA * field - PROJ_BETA * PROJ_ETA))
        height[i - REACH, r - REACH] = jnp.where(inside, value, OUTSIDE)

    sweep(cells, 1, keep(first))
    sweep(first, 2, keep(second))
    sweep(second, 3, project)
    for k in range(15):
        to_down[pl.ds(MARGIN_AT[k], 15 - k)] = height[k, pl.ds(k + 1, 15 - k)]
        to_up[pl.ds(MARGIN_AT[k], 15 - k)] = height[k, pl.ds(0, 15 - k)]


def chain_kernel(turn, count_tiles, *refs):
    if turn:
        up, middle, down, height, height_up, height_down, unused, printed, top, even, odd = refs
    else:
        height, height_up, height_down, unused, printed, top, even, odd = refs
    chip, core, tile = place()

    @pl.when(chip == turn)
    def run():
        inside = column_mask(core)
        lane = lane_of()
        lift_up = jnp.where(tile > 0, 0.0, OUTSIDE)
        lift_down = jnp.where(tile < count_tiles - 1, 0.0, OUTSIDE)
        if turn:
            for r in range(ROWS):
                even[r] = up[r] + TINY
                even[ROWS + r] = middle[r] + TINY
                even[2 * ROWS + r] = down[r] + TINY
        else:
            ones = jnp.where(inside, math.exp(SHARPNESS), TINY)
            ones_up = jnp.where(tile > 0, ones, TINY)
            ones_down = jnp.where(tile < count_tiles - 1, ones, TINY)
            for r in range(ROWS):
                even[r] = ones_up
                even[ROWS + r] = ones
                even[2 * ROWS + r] = ones_down
        level = HALF * math.sqrt(SMOOTH_EPS)
        for k in range(LAYERS):
            source, target = (even, odd) if k % 2 == 0 else (odd, even)
            for j in range(k + 1, 47 - k):
                total = source[j - 1] + source[j] + source[j + 1]
                total = total + pltpu.roll(total, 1, 1) + pltpu.roll(total, LANES - 1, 1)
                support = jnp.log(total) * (0.5 / math.log(2.0)) - 0.5 * math.log2(9.0)
                if j < ROWS:
                    blue = height_up[MARGIN_AT[k] + j - 1 - k] + lift_up
                elif j < 2 * ROWS:
                    blue = height[k, j - ROWS]
                else:
                    blue = height_down[MARGIN_AT[k] + j - 2 * ROWS] + lift_down
                gap = blue - support
                square = gap * gap + level * level
                value = (blue + support + level) - square * lax.rsqrt(square)
                weight = jnp.exp2(value)
                if ROWS <= j < 2 * ROWS:
                    printed[k, j - ROWS] = value
                if k < LAYERS - 1:
                    target[j] = weight
                else:
                    before = pltpu.roll(pltpu.roll(weight, 1, 0), LANES - STRIDE, 1)
                    after = pltpu.roll(pltpu.roll(weight, FOLDS - 1, 0), STRIDE, 1)
                    weight = jnp.where(lane < HALO, before, weight)
                    weight = jnp.where(lane >= HALO + STRIDE, after, weight)
                    top[j - ROWS] = jnp.where(inside, weight, 0.0)


def unfold_kernel(scale, folded, own, partner):
    unused, core, unused = place()
    lane = lane_of()

    def unfold(target, base):
        def layer(i, carry):
            for group in range(2):
                row = ((base + i) * ROWS + 8 * group) * FOLDS
                blocks = [folded[pl.ds(row + s, 8, stride=FOLDS), :] * scale for s in range(FOLDS)]
                for a in range(5):
                    tile = None
                    for s in range(FOLDS):
                        low = max(LANES * a, STRIDE * s)
                        if low >= min(LANES * a + LANES, STRIDE * s + STRIDE):
                            continue
                        piece = pltpu.roll(blocks[s], (STRIDE * s - LANES * a - HALO) % LANES, 1)
                        tile = piece if tile is None else jnp.where(lane >= low - LANES * a, piece, tile)

                    def store(at, tile=tile):
                        target[i, pl.ds(8 * group, 8), pl.ds(at, LANES)] = tile

                    if a == 0:
                        pl.when(core == 0)(functools.partial(store, 0))
                    elif a == 4:
                        pl.when(core == 1)(functools.partial(store, 3 * LANES))
                    else:
                        store(pl.multiple_of(LANES * (a - core), LANES))
            return carry

        lax.fori_loop(0, 8, layer, 0)

    unfold(own, 8 * core)
    unfold(partner, 8 * (1 - core))


def call(kernel, name, outs, operands, scratch=(), aliases=None):
    held = [pltpu.with_memory_space_constraint(x, pltpu.VMEM) for x in operands]
    vmem = pl.BlockSpec(memory_space=pltpu.VMEM)
    return pl.pallas_call(
        kernel,
        name=name,
        out_shape=[pltpu.VMEM(shape, jnp.float32) for shape in outs],
        in_specs=[vmem] * len(held),
        out_specs=[vmem] * len(outs),
        scratch_shapes=[pltpu.VMEM(shape, jnp.float32) for shape in scratch],
        input_output_aliases=aliases or {},
        compiler_params=pltpu.CompilerParams(vmem_limit_bytes=24 * 1024 * 1024),
    )(*held)


def local(design):
    slabs = lax.axis_size("gz")
    tiles = lax.axis_size("xy")
    chips = slabs // 2
    unused, core, unused = place()

    def at(slab, tile):
        return slab * tiles + tile

    def swap(block):
        return lax.ppermute(block, "gz", [(i, i ^ 1) for i in range(slabs)])

    def from_up(block):
        return lax.ppermute(block, "xy", [(i, i + 1) for i in range(tiles - 1)])

    def from_down(block):
        return lax.ppermute(block, "xy", [(i + 1, i) for i in range(tiles - 1)])

    rim = jnp.where(core == 0, design[:REACH], design[8 - REACH :])
    left, right = design[:, :, :PART], design[:, :, 1024 - PART :]
    rim_left, rim_right = rim[:, :, :PART], rim[:, :, 1024 - PART :]
    crossing = [(i, j) for k in range(1, chips) for i, j in ((2 * k - 1, 2 * k), (2 * k, 2 * k - 1))]
    straight = [(i, j) for k in range(1, chips) for i, j in ((2 * k - 1, 2 * k + 1), (2 * k, 2 * k - 2))]
    near = lax.ppermute(jnp.where(core == 0, rim_right, rim_left), "gz", crossing)
    far = lax.ppermute(jnp.where(core == 0, rim_left, rim_right), "gz", straight)
    partner = swap(jnp.where(core == 0, right, left))
    block = (FOLDS, LANES)
    folded, to_down, to_up = call(
        fold_kernel,
        "fold",
        [(22 * ROWS * FOLDS, LANES), (SIDE, *block), (SIDE, *block)],
        [design, partner, near, far],
    )
    height, to_down, to_up = call(
        functools.partial(filter_kernel, chips, tiles),
        "filter",
        [(LAYERS, ROWS, *block), (MARGIN, *block), (MARGIN, *block)],
        [folded.reshape(22, ROWS, *block), from_up(to_down), from_down(to_up)],
        scratch=[(22, ROWS + 2 * REACH, *block)] * 3,
    )
    height_up, height_down = from_up(to_down), from_down(to_up)

    def spread(folded, scale, name):
        own, other = call(
            functools.partial(unfold_kernel, scale),
            name,
            [(8, ROWS, 512), (8, ROWS, 512)],
            [folded.reshape(LAYERS * ROWS * FOLDS, LANES)],
        )
        other = swap(other)
        return jnp.where(
            core == 0, jnp.concatenate([own, other], axis=2), jnp.concatenate([other, own], axis=2)
        )

    printed = jnp.zeros((LAYERS, ROWS, *block), jnp.float32)
    received = []
    for turn in range(chips):
        operands = [*received, height, height_up, height_down, printed]
        printed, top = call(
            functools.partial(chain_kernel, turn, tiles),
            "chain",
            [(LAYERS, ROWS, *block), (ROWS, *block)],
            operands,
            scratch=[(48, *block)] * 2,
            aliases={len(operands) - 1: 0},
        )
        if turn < chips - 1:
            received = [
                lax.ppermute(
                    top,
                    AXES,
                    [
                        (at(2 * turn + c, t), at(2 * turn + 2 + c, t + away))
                        for c in range(2)
                        for t in range(tiles)
                        if 0 <= t + away < tiles
                    ],
                )
                for away in (1, 0, -1)
            ]
        if turn == 0:
            blueprint = spread(height, 1.0 / HALF, "blueprint")
    return blueprint, spread(printed, 0.5 / HALF, "printed")


def solution(mesh):
    spec = P("gz", "xy", None)
    return jax.shard_map(local, mesh=mesh, in_specs=(spec,), out_specs=(spec, spec), check_vma=False)
```

```python
import functools
import math

import jax
import jax.numpy as jnp
from jax import lax
from jax.experimental import pallas as pl
from jax.experimental.pallas import tpu as pltpu
from jax.sharding import PartitionSpec as P

LAYERS = 16
ROWS = 16
FOLDS = 8
LANES = 128
STRIDE = 80
HALO = 24
REACH = 3
PART = 768
AXES = ("gz", "xy")

FILTER_R2 = 4.0
PROJ_BETA = 8.0
PROJ_ETA = 0.5
SHARPNESS = 16.0
SMOOTH_EPS = 0.0001
HALF = 0.5 * SHARPNESS / math.log(2.0)
OUTSIDE = -50.0
TINY = 2.0**-100
MARGIN_AT = [sum(15 - j for j in range(k)) for k in range(16)]
MARGIN = MARGIN_AT[15]
SIDE = 20 + 18 + 16


def place():
    slab = lax.axis_index("gz")
    return lax.div(slab, 2), lax.rem(slab, 2), lax.axis_index("xy")


def lane_of(shape=(FOLDS, LANES)):
    return lax.broadcasted_iota(jnp.int32, shape, len(shape) - 1)


def column_mask(core):
    fold = lax.broadcasted_iota(jnp.int32, (FOLDS, LANES), 0)
    column = 384 * core + STRIDE * fold + lane_of() - HALO
    return (column >= 0) & (column < 1024)


def fold_kernel(own, partner, near, far, out, to_down, to_up):
    unused, core, unused = place()
    lane = lane_of()

    def fold(source, start, base, count):
        def layer(i, carry):
            for group in range(2):
                tiles = []
                for a in range(7):
                    at = jnp.clip(a - 1 + core, 0, 5) * LANES + start
                    tile = source[i, pl.ds(8 * group, 8), pl.ds(pl.multiple_of(at, LANES), LANES)]
                    if a == 0:
                        tile = jnp.where(core == 0, 0.0, tile)
                    if a == 6:
                        tile = jnp.where(core == 1, 0.0, tile)
                    tiles.append(tile)
                for s in range(FOLDS):
                    a, shift = divmod(LANES - HALO + STRIDE * s, LANES)
                    block = tiles[a]
                    if shift:
                        first = pltpu.roll(tiles[a], LANES - shift, 1)
                        second = pltpu.roll(tiles[a + 1], LANES - shift, 1)
                        block = jnp.where(lane < LANES - shift, first, second)
                    row = ((base + i) * ROWS + 8 * group) * FOLDS
                    out[pl.ds(row + s, 8, stride=FOLDS), :] = block
            return carry

        lax.fori_loop(0, count, layer, 0, unroll=count)

    fold(own, 256 * core, REACH + 8 * core, 8)
    fold(partner, 0, REACH + 8 * (1 - core), 8)
    fold(near, 0, 19 * core, REACH)
    fold(far, 0, 19 * (1 - core), REACH)
    at = 0
    for away in range(REACH):
        for i in range(1 + away, 21 - away):
            to_down[at] = out[pl.ds((i * ROWS + 15 - away) * FOLDS, FOLDS), :]
            to_up[at] = out[pl.ds((i * ROWS + away) * FOLDS, FOLDS), :]
            at += 1


def filter_kernel(count_chips, count_tiles, own, up, down, height, to_down, to_up, cells, first, second):
    chip, core, tile = place()
    inside = column_mask(core)
    scale = jnp.where(inside, 1.0 / (1.0 + 6.0 * FILTER_R2), 0.0)
    above = jnp.where(tile > 0, 1.0, 0.0)
    below = jnp.where(tile < count_tiles - 1, 1.0, 0.0)

    def gather(i, carry):
        cells[i, pl.ds(REACH, ROWS)] = own[i]
        return carry

    lax.fori_loop(0, 22, gather, 0, unroll=22)
    at = 0
    for away in range(REACH):
        for i in range(1 + away, 21 - away):
            cells[i, REACH - 1 - away] = up[at]
            cells[i, REACH + ROWS + away] = down[at]
            at += 1

    def sweep(source, step, store):
        rim = REACH - step

        def layer(i, rows):
            held = jnp.where(((chip == 0) & (i < REACH)) | ((chip == count_chips - 1) & (i >= REACH + LAYERS)), 0.0, scale)
            for r in rows:
                middle = source[i, r]
                total = source[i - 1, r] + source[i + 1, r] + source[i, r - 1] + source[i, r + 1]
                total = total + pltpu.roll(middle, 1, 1) + pltpu.roll(middle, LANES - 1, 1)
                factor = held
                if r < REACH:
                    factor = held * above
                if r >= REACH + ROWS:
                    factor = held * below
                store(i, r, (cells[i, r] + FILTER_R2 * total) * factor)

        def body(i, carry):
            layer(i, range(REACH - rim, REACH + ROWS + rim))
            return carry

        for away in range(rim):
            for i in (REACH - rim + away, REACH + LAYERS + rim - 1 - away):
                layer(i, range(REACH - away, REACH + ROWS + away))
        lax.fori_loop(REACH, REACH + LAYERS, body, 0, unroll=LAYERS)

    def keep(target):
        def store(i, r, value):
            target[i, r] = value

        return store

    base = math.tanh(PROJ_BETA * PROJ_ETA)
    gain = HALF / (math.tanh(PROJ_BETA * PROJ_ETA) + math.tanh(PROJ_BETA * (1.0 - PROJ_ETA)))

    def project(i, r, field):
        value = gain * (base + jnp.tanh(PROJ_BETA * field - PROJ_BETA * PROJ_ETA))
        height[i - REACH, r - REACH] = jnp.where(inside, value, OUTSIDE)

    sweep(cells, 1, keep(first))
    sweep(first, 2, keep(second))
    sweep(second, 3, project)
    for k in range(15):
        to_down[pl.ds(MARGIN_AT[k], 15 - k)] = height[k, pl.ds(k + 1, 15 - k)]
        to_up[pl.ds(MARGIN_AT[k], 15 - k)] = height[k, pl.ds(0, 15 - k)]


def chain_kernel(turn, count_tiles, *refs):
    if turn:
        up, middle, down, height, height_up, height_down, unused, printed, top, even, odd = refs
    else:
        height, height_up, height_down, unused, printed, top, even, odd = refs
    chip, core, tile = place()

    @pl.when(chip == turn)
    def run():
        inside = column_mask(core)
        lane = lane_of()
        lift_up = jnp.where(tile > 0, 0.0, OUTSIDE)
        lift_down = jnp.where(tile < count_tiles - 1, 0.0, OUTSIDE)
        if turn:
            for r in range(ROWS):
                even[r] = up[r] + TINY
                even[ROWS + r] = middle[r] + TINY
                even[2 * ROWS + r] = down[r] + TINY
        else:
            ones = jnp.where(inside, math.exp(SHARPNESS), TINY)
            ones_up = jnp.where(tile > 0, ones, TINY)
            ones_down = jnp.where(tile < count_tiles - 1, ones, TINY)
            for r in range(ROWS):
                even[r] = ones_up
                even[ROWS + r] = ones
                even[2 * ROWS + r] = ones_down
        level = HALF * math.sqrt(SMOOTH_EPS)
        for k in range(LAYERS):
            source, target = (even, odd) if k % 2 == 0 else (odd, even)
            for j in range(k + 1, 47 - k):
                total = source[j - 1] + source[j] + source[j + 1]
                total = total + pltpu.roll(total, 1, 1) + pltpu.roll(total, LANES - 1, 1)
                support = jnp.log(total) * (0.5 / math.log(2.0)) - 0.5 * math.log2(9.0)
                if j < ROWS:
                    blue = height_up[MARGIN_AT[k] + j - 1 - k] + lift_up
                elif j < 2 * ROWS:
                    blue = height[k, j - ROWS]
                else:
                    blue = height_down[MARGIN_AT[k] + j - 2 * ROWS] + lift_down
                gap = blue - support
                square = gap * gap + level * level
                value = (blue + support + level) - square * lax.rsqrt(square)
                weight = jnp.exp2(value)
                if ROWS <= j < 2 * ROWS:
                    printed[k, j - ROWS] = value
                if k < LAYERS - 1:
                    target[j] = weight
                else:
                    before = pltpu.roll(pltpu.roll(weight, 1, 0), LANES - STRIDE, 1)
                    after = pltpu.roll(pltpu.roll(weight, FOLDS - 1, 0), STRIDE, 1)
                    weight = jnp.where(lane < HALO, before, weight)
                    weight = jnp.where(lane >= HALO + STRIDE, after, weight)
                    top[j - ROWS] = jnp.where(inside, weight, 0.0)


def unfold_kernel(scale, folded, own, partner):
    unused, core, unused = place()
    lane = lane_of()

    def unfold(target, base):
        def layer(i, carry):
            for group in range(2):
                row = ((base + i) * ROWS + 8 * group) * FOLDS
                blocks = [folded[pl.ds(row + s, 8, stride=FOLDS), :] * scale for s in range(FOLDS)]
                tiles = []
                for a in range(5):
                    tile = None
                    for s in range(FOLDS):
                        low = max(LANES * a, STRIDE * s)
                        if low >= min(LANES * a + LANES, STRIDE * s + STRIDE):
                            continue
                        piece = pltpu.roll(blocks[s], (STRIDE * s - LANES * a - HALO) % LANES, 1)
                        tile = piece if tile is None else jnp.where(lane >= low - LANES * a, piece, tile)
                    tiles.append(tile)
                for a in range(4):
                    target[i, pl.ds(8 * group, 8), pl.ds(LANES * a, LANES)] = jnp.where(core == 0, tiles[a], tiles[a + 1])
            return carry

        lax.fori_loop(0, 8, layer, 0, unroll=8)

    unfold(own, 8 * core)
    unfold(partner, 8 * (1 - core))


def call(kernel, name, outs, operands, scratch=(), aliases=None):
    held = [pltpu.with_memory_space_constraint(x, pltpu.VMEM) for x in operands]
    vmem = pl.BlockSpec(memory_space=pltpu.VMEM)
    return pl.pallas_call(
        kernel,
        name=name,
        out_shape=[pltpu.VMEM(shape, jnp.float32) for shape in outs],
        in_specs=[vmem] * len(held),
        out_specs=[vmem] * len(outs),
        scratch_shapes=[pltpu.VMEM(shape, jnp.float32) for shape in scratch],
        input_output_aliases=aliases or {},
        compiler_params=pltpu.CompilerParams(vmem_limit_bytes=24 * 1024 * 1024),
    )(*held)


def local(design):
    slabs = lax.axis_size("gz")
    tiles = lax.axis_size("xy")
    chips = slabs // 2
    unused, core, unused = place()

    def at(slab, tile):
        return slab * tiles + tile

    def swap(block):
        return lax.ppermute(block, "gz", [(i, i ^ 1) for i in range(slabs)])

    def from_up(block):
        return lax.ppermute(block, "xy", [(i, i + 1) for i in range(tiles - 1)])

    def from_down(block):
        return lax.ppermute(block, "xy", [(i + 1, i) for i in range(tiles - 1)])

    rim = jnp.where(core == 0, design[:REACH], design[8 - REACH :])
    left, right = design[:, :, :PART], design[:, :, 1024 - PART :]
    rim_left, rim_right = rim[:, :, :PART], rim[:, :, 1024 - PART :]
    crossing = [(i, j) for k in range(1, chips) for i, j in ((2 * k - 1, 2 * k), (2 * k, 2 * k - 1))]
    straight = [(i, j) for k in range(1, chips) for i, j in ((2 * k - 1, 2 * k + 1), (2 * k, 2 * k - 2))]
    near = lax.ppermute(jnp.where(core == 0, rim_right, rim_left), "gz", crossing)
    far = lax.ppermute(jnp.where(core == 0, rim_left, rim_right), "gz", straight)
    partner = swap(jnp.where(core == 0, right, left))
    block = (FOLDS, LANES)
    folded, to_down, to_up = call(
        fold_kernel,
        "fold",
        [(22 * ROWS * FOLDS, LANES), (SIDE, *block), (SIDE, *block)],
        [design, partner, near, far],
    )
    height, to_down, to_up = call(
        functools.partial(filter_kernel, chips, tiles),
        "filter",
        [(LAYERS, ROWS, *block), (MARGIN, *block), (MARGIN, *block)],
        [folded.reshape(22, ROWS, *block), from_up(to_down), from_down(to_up)],
        scratch=[(22, ROWS + 2 * REACH, *block)] * 3,
    )
    height_up, height_down = from_up(to_down), from_down(to_up)

    def spread(folded, scale, name):
        own, other = call(
            functools.partial(unfold_kernel, scale),
            name,
            [(8, ROWS, 512), (8, ROWS, 512)],
            [folded.reshape(LAYERS * ROWS * FOLDS, LANES)],
        )
        other = swap(other)
        return jnp.where(
            core == 0, jnp.concatenate([own, other], axis=2), jnp.concatenate([other, own], axis=2)
        )

    printed = jnp.zeros((LAYERS, ROWS, *block), jnp.float32)
    received = []
    for turn in range(chips):
        operands = [*received, height, height_up, height_down, printed]
        printed, top = call(
            functools.partial(chain_kernel, turn, tiles),
            "chain",
            [(LAYERS, ROWS, *block), (ROWS, *block)],
            operands,
            scratch=[(48, *block)] * 2,
            aliases={len(operands) - 1: 0},
        )
        if turn < chips - 1:
            received = [
                lax.ppermute(
                    top,
                    AXES,
                    [
                        (at(2 * turn + c, t), at(2 * turn + 2 + c, t + away))
                        for c in range(2)
                        for t in range(tiles)
                        if 0 <= t + away < tiles
                    ],
                )
                for away in (1, 0, -1)
            ]
        if turn == 0:
            shown, unused = lax.optimization_barrier((height, top))
            blueprint = spread(shown, 1.0 / HALF, "blueprint")
            printed, blueprint = lax.optimization_barrier((printed, blueprint))
    return blueprint, spread(printed, 0.5 / HALF, "printed")


def solution(mesh):
    spec = P("gz", "xy", None)
    return jax.shard_map(local, mesh=mesh, in_specs=(spec,), out_specs=(spec, spec), check_vma=False)
```

```python
import functools
import math

import jax
import jax.numpy as jnp
from jax import lax
from jax.experimental import pallas as pl
from jax.experimental.pallas import tpu as pltpu
from jax.sharding import PartitionSpec as P

LAYERS = 16
ROWS = 16
FOLDS = 8
LANES = 128
STRIDE = 80
HALO = 24
REACH = 3
PART = 768
AXES = ("gz", "xy")

FILTER_R2 = 4.0
PROJ_BETA = 8.0
PROJ_ETA = 0.5
SHARPNESS = 16.0
SMOOTH_EPS = 0.0001
HALF = 0.5 * SHARPNESS / math.log(2.0)
OUTSIDE = -50.0
TINY = 2.0**-100
MARGIN_AT = [sum(15 - j for j in range(k)) for k in range(16)]
MARGIN = MARGIN_AT[15]
SIDE = 20 + 18 + 16


def place():
    slab = lax.axis_index("gz")
    return lax.div(slab, 2), lax.rem(slab, 2), lax.axis_index("xy")


def lane_of(shape=(FOLDS, LANES)):
    return lax.broadcasted_iota(jnp.int32, shape, len(shape) - 1)


def column_mask(core):
    fold = lax.broadcasted_iota(jnp.int32, (FOLDS, LANES), 0)
    column = 384 * core + STRIDE * fold + lane_of() - HALO
    return (column >= 0) & (column < 1024)


def fold_kernel(own, partner, near, far, out, to_down, to_up):
    unused, core, unused = place()
    lane = lane_of()

    def fold(source, start, base, count):
        def layer(i, carry):
            for group in range(2):
                tiles = []
                for a in range(7):
                    at = jnp.clip(a - 1 + core, 0, 5) * LANES + start
                    tile = source[i, pl.ds(8 * group, 8), pl.ds(pl.multiple_of(at, LANES), LANES)]
                    if a == 0:
                        tile = jnp.where(core == 0, 0.0, tile)
                    if a == 6:
                        tile = jnp.where(core == 1, 0.0, tile)
                    tiles.append(tile)
                for s in range(FOLDS):
                    a, shift = divmod(LANES - HALO + STRIDE * s, LANES)
                    block = tiles[a]
                    if shift:
                        first = pltpu.roll(tiles[a], LANES - shift, 1)
                        second = pltpu.roll(tiles[a + 1], LANES - shift, 1)
                        block = jnp.where(lane < LANES - shift, first, second)
                    row = ((base + i) * ROWS + 8 * group) * FOLDS
                    out[pl.ds(row + s, 8, stride=FOLDS), :] = block
            return carry

        lax.fori_loop(0, count, layer, 0, unroll=count)

    fold(own, 256 * core, REACH + 8 * core, 8)
    fold(partner, 0, REACH + 8 * (1 - core), 8)
    fold(near, 0, 19 * core, REACH)
    fold(far, 0, 19 * (1 - core), REACH)
    at = 0
    for away in range(REACH):
        for i in range(1 + away, 21 - away):
            to_down[at] = out[pl.ds((i * ROWS + 15 - away) * FOLDS, FOLDS), :]
            to_up[at] = out[pl.ds((i * ROWS + away) * FOLDS, FOLDS), :]
            at += 1


def filter_kernel(count_chips, count_tiles, own, up, down, height, to_down, to_up, cells, first, second):
    chip, core, tile = place()
    inside = column_mask(core)
    scale = jnp.where(inside, 1.0 / (1.0 + 6.0 * FILTER_R2), 0.0)
    above = jnp.where(tile > 0, 1.0, 0.0)
    below = jnp.where(tile < count_tiles - 1, 1.0, 0.0)

    def gather(i, carry):
        cells[i, pl.ds(REACH, ROWS)] = own[i]
        return carry

    lax.fori_loop(0, 22, gather, 0, unroll=22)
    at = 0
    for away in range(REACH):
        for i in range(1 + away, 21 - away):
            cells[i, REACH - 1 - away] = up[at]
            cells[i, REACH + ROWS + away] = down[at]
            at += 1

    def sweep(source, step, store):
        rim = REACH - step

        def layer(i, rows):
            held = jnp.where(((chip == 0) & (i < REACH)) | ((chip == count_chips - 1) & (i >= REACH + LAYERS)), 0.0, scale)
            for r in rows:
                middle = source[i, r]
                total = source[i - 1, r] + source[i + 1, r] + source[i, r - 1] + source[i, r + 1]
                total = total + pltpu.roll(middle, 1, 1) + pltpu.roll(middle, LANES - 1, 1)
                factor = held
                if r < REACH:
                    factor = held * above
                if r >= REACH + ROWS:
                    factor = held * below
                store(i, r, (cells[i, r] + FILTER_R2 * total) * factor)

        def body(i, carry):
            layer(i, range(REACH - rim, REACH + ROWS + rim))
            return carry

        for away in range(rim):
            for i in (REACH - rim + away, REACH + LAYERS + rim - 1 - away):
                layer(i, range(REACH - away, REACH + ROWS + away))
        lax.fori_loop(REACH, REACH + LAYERS, body, 0, unroll=LAYERS)

    def keep(target):
        def store(i, r, value):
            target[i, r] = value

        return store

    base = math.tanh(PROJ_BETA * PROJ_ETA)
    gain = HALF / (math.tanh(PROJ_BETA * PROJ_ETA) + math.tanh(PROJ_BETA * (1.0 - PROJ_ETA)))

    def project(i, r, field):
        value = gain * (base + jnp.tanh(PROJ_BETA * field - PROJ_BETA * PROJ_ETA))
        height[i - REACH, r - REACH] = jnp.where(inside, value, OUTSIDE)

    sweep(cells, 1, keep(first))
    sweep(first, 2, keep(second))
    sweep(second, 3, project)
    for k in range(15):
        to_down[pl.ds(MARGIN_AT[k], 15 - k)] = height[k, pl.ds(k + 1, 15 - k)]
        to_up[pl.ds(MARGIN_AT[k], 15 - k)] = height[k, pl.ds(0, 15 - k)]


def chain_kernel(turn, count_tiles, *refs):
    if turn:
        up, down, middle, height, height_up, height_down, unused, printed, top, even, odd = refs
    else:
        height, height_up, height_down, unused, printed, top, even, odd = refs
    chip, core, tile = place()

    @pl.when(chip == turn)
    def run():
        inside = column_mask(core)
        lane = lane_of()
        lift_up = jnp.where(tile > 0, 0.0, OUTSIDE)
        lift_down = jnp.where(tile < count_tiles - 1, 0.0, OUTSIDE)
        if turn:
            for r in range(ROWS):
                even[r] = up[r] + TINY
                even[ROWS + r] = middle[r] + TINY
                even[2 * ROWS + r] = down[r] + TINY
        else:
            ones = jnp.where(inside, math.exp(SHARPNESS), TINY)
            ones_up = jnp.where(tile > 0, ones, TINY)
            ones_down = jnp.where(tile < count_tiles - 1, ones, TINY)
            for r in range(ROWS):
                even[r] = ones_up
                even[ROWS + r] = ones
                even[2 * ROWS + r] = ones_down
        level = HALF * math.sqrt(SMOOTH_EPS)
        for k in range(LAYERS):
            source, target = (even, odd) if k % 2 == 0 else (odd, even)
            for j in range(k + 1, 47 - k):
                total = source[j - 1] + source[j] + source[j + 1]
                total = total + pltpu.roll(total, 1, 1) + pltpu.roll(total, LANES - 1, 1)
                support = jnp.log(total) * (0.5 / math.log(2.0)) - 0.5 * math.log2(9.0)
                if j < ROWS:
                    blue = height_up[MARGIN_AT[k] + j - 1 - k] + lift_up
                elif j < 2 * ROWS:
                    blue = height[k, j - ROWS]
                else:
                    blue = height_down[MARGIN_AT[k] + j - 2 * ROWS] + lift_down
                gap = blue - support
                square = gap * gap + level * level
                value = (blue + support + level) - square * lax.rsqrt(square)
                weight = jnp.exp2(value)
                if ROWS <= j < 2 * ROWS:
                    printed[k, j - ROWS] = value
                if k < LAYERS - 1:
                    target[j] = weight
                else:
                    before = pltpu.roll(pltpu.roll(weight, 1, 0), LANES - STRIDE, 1)
                    after = pltpu.roll(pltpu.roll(weight, FOLDS - 1, 0), STRIDE, 1)
                    weight = jnp.where(lane < HALO, before, weight)
                    weight = jnp.where(lane >= HALO + STRIDE, after, weight)
                    top[j - ROWS] = jnp.where(inside, weight, 0.0)


def unfold_kernel(scale, folded, own, partner):
    unused, core, unused = place()
    lane = lane_of()

    def unfold(target, base):
        def layer(i, carry):
            for group in range(2):
                row = ((base + i) * ROWS + 8 * group) * FOLDS
                blocks = [folded[pl.ds(row + s, 8, stride=FOLDS), :] * scale for s in range(FOLDS)]
                tiles = []
                for a in range(5):
                    tile = None
                    for s in range(FOLDS):
                        low = max(LANES * a, STRIDE * s)
                        if low >= min(LANES * a + LANES, STRIDE * s + STRIDE):
                            continue
                        piece = pltpu.roll(blocks[s], (STRIDE * s - LANES * a - HALO) % LANES, 1)
                        tile = piece if tile is None else jnp.where(lane >= low - LANES * a, piece, tile)
                    tiles.append(tile)
                for a in range(4):
                    target[i, pl.ds(8 * group, 8), pl.ds(LANES * a, LANES)] = jnp.where(core == 0, tiles[a], tiles[a + 1])
            return carry

        lax.fori_loop(0, 8, layer, 0, unroll=8)

    unfold(own, 8 * core)
    unfold(partner, 8 * (1 - core))


def call(kernel, name, outs, operands, scratch=(), aliases=None):
    held = [pltpu.with_memory_space_constraint(x, pltpu.VMEM) for x in operands]
    vmem = pl.BlockSpec(memory_space=pltpu.VMEM)
    return pl.pallas_call(
        kernel,
        name=name,
        out_shape=[pltpu.VMEM(shape, jnp.float32) for shape in outs],
        in_specs=[vmem] * len(held),
        out_specs=[vmem] * len(outs),
        scratch_shapes=[pltpu.VMEM(shape, jnp.float32) for shape in scratch],
        input_output_aliases=aliases or {},
        compiler_params=pltpu.CompilerParams(vmem_limit_bytes=24 * 1024 * 1024),
    )(*held)


def local(design):
    slabs = lax.axis_size("gz")
    tiles = lax.axis_size("xy")
    chips = slabs // 2
    unused, core, unused = place()

    def at(slab, tile):
        return slab * tiles + tile

    def swap(block):
        return lax.ppermute(block, "gz", [(i, i ^ 1) for i in range(slabs)])

    def from_up(block):
        return lax.ppermute(block, "xy", [(i, i + 1) for i in range(tiles - 1)])

    def from_down(block):
        return lax.ppermute(block, "xy", [(i + 1, i) for i in range(tiles - 1)])

    rim = jnp.where(core == 0, design[:REACH], design[8 - REACH :])
    left, right = design[:, :, :PART], design[:, :, 1024 - PART :]
    rim_left, rim_right = rim[:, :, :PART], rim[:, :, 1024 - PART :]
    crossing = [(i, j) for k in range(1, chips) for i, j in ((2 * k - 1, 2 * k), (2 * k, 2 * k - 1))]
    straight = [(i, j) for k in range(1, chips) for i, j in ((2 * k - 1, 2 * k + 1), (2 * k, 2 * k - 2))]
    near = lax.ppermute(jnp.where(core == 0, rim_right, rim_left), "gz", crossing)
    far = lax.ppermute(jnp.where(core == 0, rim_left, rim_right), "gz", straight)
    partner = swap(jnp.where(core == 0, right, left))
    block = (FOLDS, LANES)
    folded, to_down, to_up = call(
        fold_kernel,
        "fold",
        [(22 * ROWS * FOLDS, LANES), (SIDE, *block), (SIDE, *block)],
        [design, partner, near, far],
    )
    height, to_down, to_up = call(
        functools.partial(filter_kernel, chips, tiles),
        "filter",
        [(LAYERS, ROWS, *block), (MARGIN, *block), (MARGIN, *block)],
        [folded.reshape(22, ROWS, *block), from_up(to_down), from_down(to_up)],
        scratch=[(22, ROWS + 2 * REACH, *block)] * 3,
    )
    height_up, height_down = from_up(to_down), from_down(to_up)

    def spread(folded, scale, name):
        own, other = call(
            functools.partial(unfold_kernel, scale),
            name,
            [(8, ROWS, 512), (8, ROWS, 512)],
            [folded.reshape(LAYERS * ROWS * FOLDS, LANES)],
        )
        return own, swap(other)

    def assemble(own, other):
        return jnp.where(
            core == 0, jnp.concatenate([own, other], axis=2), jnp.concatenate([other, own], axis=2)
        )

    shown, height_up = lax.optimization_barrier((height, height_up))
    shown = spread(shown, 1.0 / HALF, "blueprint")
    height, shown = lax.optimization_barrier((height, shown))
    printed = jnp.zeros((LAYERS, ROWS, *block), jnp.float32)
    received = []
    for turn in range(chips):
        operands = [*received, height, height_up, height_down, printed]
        printed, top = call(
            functools.partial(chain_kernel, turn, tiles),
            "chain",
            [(LAYERS, ROWS, *block), (ROWS, *block)],
            operands,
            scratch=[(48, *block)] * 2,
            aliases={len(operands) - 1: 0},
        )
        if turn < chips - 1:
            received = [
                lax.ppermute(
                    top,
                    AXES,
                    [
                        (at(2 * turn + c, t), at(2 * turn + 2 + c, t + away))
                        for c in range(2)
                        for t in range(tiles)
                        if 0 <= t + away < tiles
                    ],
                )
                for away in (1, -1, 0)
            ]
        if turn == 0:
            printed, blueprint = lax.optimization_barrier((printed, assemble(*shown)))
    return blueprint, assemble(*spread(printed, 0.5 / HALF, "printed"))


def solution(mesh):
    spec = P("gz", "xy", None)
    return jax.shard_map(local, mesh=mesh, in_specs=(spec,), out_specs=(spec, spec), check_vma=False)
```

```python
import functools
import math

import jax
import jax.numpy as jnp
from jax import lax
from jax.experimental import pallas as pl
from jax.experimental.pallas import tpu as pltpu
from jax.sharding import PartitionSpec as P

LAYERS = 16
ROWS = 16
FOLDS = 8
LANES = 128
STRIDE = 80
HALO = 24
REACH = 3
PART = 768
AXES = ("gz", "xy")

FILTER_R2 = 4.0
PROJ_BETA = 8.0
PROJ_ETA = 0.5
SHARPNESS = 16.0
SMOOTH_EPS = 0.0001
HALF = 0.5 * SHARPNESS / math.log(2.0)
OUTSIDE = -50.0
TINY = 2.0**-100
MARGIN_AT = [sum(15 - j for j in range(k)) for k in range(16)]
MARGIN = MARGIN_AT[15]
SIDE = 20 + 18 + 16


def place():
    slab = lax.axis_index("gz")
    return lax.div(slab, 2), lax.rem(slab, 2), lax.axis_index("xy")


def lane_of(shape=(FOLDS, LANES)):
    return lax.broadcasted_iota(jnp.int32, shape, len(shape) - 1)


def column_mask(core):
    fold = lax.broadcasted_iota(jnp.int32, (FOLDS, LANES), 0)
    column = 384 * core + STRIDE * fold + lane_of() - HALO
    return (column >= 0) & (column < 1024)


def fold_rows(tiles, lane, store):
    for s in range(FOLDS):
        a, shift = divmod(LANES - HALO + STRIDE * s, LANES)
        block = tiles[a]
        if shift:
            first = pltpu.roll(tiles[a], LANES - shift, 1)
            second = pltpu.roll(tiles[a + 1], LANES - shift, 1)
            block = jnp.where(lane < LANES - shift, first, second)
        store(s, block)


def unfold_rows(blocks, lane):
    tiles = []
    for a in range(5):
        tile = None
        for s in range(FOLDS):
            low = max(LANES * a, STRIDE * s)
            if low >= min(LANES * a + LANES, STRIDE * s + STRIDE):
                continue
            piece = pltpu.roll(blocks[s], (STRIDE * s - LANES * a - HALO) % LANES, 1)
            tile = piece if tile is None else jnp.where(lane >= low - LANES * a, piece, tile)
        tiles.append(tile)
    return tiles


def fold_kernel(own, partner, near, far, out, to_down, to_up):
    unused, core, unused = place()
    lane = lane_of()

    def fold(source, start, base, count):
        def layer(i, carry):
            for group in range(2):
                tiles = []
                for a in range(7):
                    at = jnp.clip(a - 1 + core, 0, 5) * LANES + start
                    tile = source[i, pl.ds(8 * group, 8), pl.ds(pl.multiple_of(at, LANES), LANES)]
                    if a == 0:
                        tile = jnp.where(core == 0, 0.0, tile)
                    if a == 6:
                        tile = jnp.where(core == 1, 0.0, tile)
                    tiles.append(tile)
                row = ((base + i) * ROWS + 8 * group) * FOLDS

                def store(s, block):
                    out[pl.ds(row + s, 8, stride=FOLDS), :] = block

                fold_rows(tiles, lane, store)
            return carry

        lax.fori_loop(0, count, layer, 0, unroll=count)

    fold(own, 256 * core, REACH + 8 * core, 8)
    fold(partner, 0, REACH + 8 * (1 - core), 8)
    fold(near, 0, 19 * core, REACH)
    fold(far, 0, 19 * (1 - core), REACH)
    at = 0
    for away in range(REACH):
        for i in range(1 + away, 21 - away):
            to_down[at] = out[pl.ds((i * ROWS + 15 - away) * FOLDS, FOLDS), :]
            to_up[at] = out[pl.ds((i * ROWS + away) * FOLDS, FOLDS), :]
            at += 1


def filter_kernel(count_chips, count_tiles, own, up, down, height, to_down, to_up, cells, first, second, packed):
    chip, core, tile = place()
    inside = column_mask(core)
    scale = jnp.where(inside, 1.0 / (1.0 + 6.0 * FILTER_R2), 0.0)
    above = jnp.where(tile > 0, 1.0, 0.0)
    below = jnp.where(tile < count_tiles - 1, 1.0, 0.0)

    def gather(i, carry):
        cells[i, pl.ds(REACH, ROWS)] = own[i]
        return carry

    lax.fori_loop(0, 22, gather, 0, unroll=22)
    at = 0
    for away in range(REACH):
        for i in range(1 + away, 21 - away):
            cells[i, REACH - 1 - away] = up[at]
            cells[i, REACH + ROWS + away] = down[at]
            at += 1

    def sweep(source, step, store):
        rim = REACH - step

        def layer(i, rows):
            held = jnp.where(((chip == 0) & (i < REACH)) | ((chip == count_chips - 1) & (i >= REACH + LAYERS)), 0.0, scale)
            for r in rows:
                middle = source[i, r]
                total = source[i - 1, r] + source[i + 1, r] + source[i, r - 1] + source[i, r + 1]
                total = total + pltpu.roll(middle, 1, 1) + pltpu.roll(middle, LANES - 1, 1)
                factor = held
                if r < REACH:
                    factor = held * above
                if r >= REACH + ROWS:
                    factor = held * below
                store(i, r, (cells[i, r] + FILTER_R2 * total) * factor)

        def body(i, carry):
            layer(i, range(REACH - rim, REACH + ROWS + rim))
            return carry

        for away in range(rim):
            for i in (REACH - rim + away, REACH + LAYERS + rim - 1 - away):
                layer(i, range(REACH - away, REACH + ROWS + away))
        lax.fori_loop(REACH, REACH + LAYERS, body, 0, unroll=LAYERS)

    def keep(target):
        def store(i, r, value):
            target[i, r] = value

        return store

    base = math.tanh(PROJ_BETA * PROJ_ETA)
    gain = HALF / (math.tanh(PROJ_BETA * PROJ_ETA) + math.tanh(PROJ_BETA * (1.0 - PROJ_ETA)))

    def project(i, r, field):
        value = gain * (base + jnp.tanh(PROJ_BETA * field - PROJ_BETA * PROJ_ETA))
        height[i - REACH, r - REACH] = jnp.where(inside, value, OUTSIDE)

    sweep(cells, 1, keep(first))
    sweep(first, 2, keep(second))
    sweep(second, 3, project)
    lane = lane_of()
    for target, low in ((to_down, 1), (to_up, 0)):
        for k in range(15):
            rows = height[k, pl.ds(low * (k + 1), 15 - k)]
            packed[pl.ds(MARGIN_AT[k] * FOLDS, (15 - k) * FOLDS), :] = rows.reshape((15 - k) * FOLDS, LANES)
        for group in range(MARGIN // 8):
            blocks = [packed[pl.ds(8 * group * FOLDS + s, 8, stride=FOLDS), :] for s in range(FOLDS)]
            for a, tile in enumerate(unfold_rows(blocks, lane)):
                target[pl.ds(8 * group, 8), pl.ds(LANES * a, LANES)] = tile


def widen_kernel(edge, rows, out):
    unused, core, tile = place()
    lane = lane_of()
    zero = jnp.zeros((8, LANES), jnp.float32)
    for group in range(MARGIN // 8):
        tiles = [rows[pl.ds(8 * group, 8), pl.ds(LANES * a, LANES)] for a in range(5)]

        def store(s, block):
            out[pl.ds(8 * group * FOLDS + s, 8, stride=FOLDS), :] = block

        fold_rows([zero, *tiles, zero], lane, store)
    inside = column_mask(core) & (tile != edge)
    for r in range(MARGIN):
        at = pl.ds(r * FOLDS, FOLDS)
        out[at, :] = jnp.where(inside, out[at, :], OUTSIDE)


def chain_kernel(turn, count_tiles, *refs):
    received, refs = (refs[:3], refs[3:]) if turn else ((), refs)
    height, height_up, height_down, unused, printed, *top, even, odd = refs
    chip, core, tile = place()

    @pl.when(chip == turn)
    def run():
        inside = column_mask(core)
        lane = lane_of()
        if turn:
            up, down, middle = received
            for r in range(ROWS):
                even[r] = up[r] + TINY
                even[ROWS + r] = middle[r] + TINY
                even[2 * ROWS + r] = down[r] + TINY
        else:
            ones = jnp.where(inside, math.exp(SHARPNESS), TINY)
            ones_up = jnp.where(tile > 0, ones, TINY)
            ones_down = jnp.where(tile < count_tiles - 1, ones, TINY)
            for r in range(ROWS):
                even[r] = ones_up
                even[ROWS + r] = ones
                even[2 * ROWS + r] = ones_down
        level = HALF * math.sqrt(SMOOTH_EPS)
        for k in range(LAYERS):
            source, target = (even, odd) if k % 2 == 0 else (odd, even)
            for j in range(k + 1, 47 - k):
                total = source[j - 1] + source[j] + source[j + 1]
                total = total + pltpu.roll(total, 1, 1) + pltpu.roll(total, LANES - 1, 1)
                support = jnp.log(total) * (0.5 / math.log(2.0)) - 0.5 * math.log2(9.0)
                if j < ROWS:
                    blue = height_up[MARGIN_AT[k] + j - 1 - k]
                elif j < 2 * ROWS:
                    blue = height[k, j - ROWS]
                else:
                    blue = height_down[MARGIN_AT[k] + j - 2 * ROWS]
                gap = blue - support
                square = gap * gap + level * level
                value = (blue + support + level) - square * lax.rsqrt(square)
                weight = jnp.exp2(value)
                if ROWS <= j < 2 * ROWS:
                    printed[k, j - ROWS] = value
                if k < LAYERS - 1:
                    target[j] = weight
                elif top:
                    before = pltpu.roll(pltpu.roll(weight, 1, 0), LANES - STRIDE, 1)
                    after = pltpu.roll(pltpu.roll(weight, FOLDS - 1, 0), STRIDE, 1)
                    weight = jnp.where(lane < HALO, before, weight)
                    weight = jnp.where(lane >= HALO + STRIDE, after, weight)
                    top[0][j - ROWS] = jnp.where(inside, weight, 0.0)


def unfold_kernel(scale, folded, own, partner):
    unused, core, unused = place()
    lane = lane_of()

    def unfold(target, base):
        def layer(i, carry):
            for group in range(2):
                row = ((base + i) * ROWS + 8 * group) * FOLDS
                blocks = [folded[pl.ds(row + s, 8, stride=FOLDS), :] * scale for s in range(FOLDS)]
                tiles = unfold_rows(blocks, lane)
                for a in range(4):
                    target[i, pl.ds(8 * group, 8), pl.ds(LANES * a, LANES)] = jnp.where(core == 0, tiles[a], tiles[a + 1])
            return carry

        lax.fori_loop(0, 8, layer, 0, unroll=8)

    unfold(own, 8 * core)
    unfold(partner, 8 * (1 - core))


def call(kernel, name, outs, operands, scratch=(), aliases=None):
    held = [pltpu.with_memory_space_constraint(x, pltpu.VMEM) for x in operands]
    vmem = pl.BlockSpec(memory_space=pltpu.VMEM)
    return pl.pallas_call(
        kernel,
        name=name,
        out_shape=[pltpu.VMEM(shape, jnp.float32) for shape in outs],
        in_specs=[vmem] * len(held),
        out_specs=[vmem] * len(outs),
        scratch_shapes=[pltpu.VMEM(shape, jnp.float32) for shape in scratch],
        input_output_aliases=aliases or {},
        compiler_params=pltpu.CompilerParams(vmem_limit_bytes=24 * 1024 * 1024),
    )(*held)


def local(design):
    slabs = lax.axis_size("gz")
    tiles = lax.axis_size("xy")
    chips = slabs // 2
    unused, core, unused = place()

    def at(slab, tile):
        return slab * tiles + tile

    def swap(block):
        return lax.ppermute(block, "gz", [(i, i ^ 1) for i in range(slabs)])

    def from_up(block):
        return lax.ppermute(block, "xy", [(i, i + 1) for i in range(tiles - 1)])

    def from_down(block):
        return lax.ppermute(block, "xy", [(i + 1, i) for i in range(tiles - 1)])

    rim = jnp.where(core == 0, design[:REACH], design[8 - REACH :])
    left, right = design[:, :, :PART], design[:, :, 1024 - PART :]
    rim_left, rim_right = rim[:, :, :PART], rim[:, :, 1024 - PART :]
    crossing = [(i, j) for k in range(1, chips) for i, j in ((2 * k - 1, 2 * k), (2 * k, 2 * k - 1))]
    straight = [(i, j) for k in range(1, chips) for i, j in ((2 * k - 1, 2 * k + 1), (2 * k, 2 * k - 2))]
    near, far, partner = lax.optimization_barrier(
        (
            jnp.where(core == 0, rim_right, rim_left),
            jnp.where(core == 0, rim_left, rim_right),
            jnp.where(core == 0, right, left),
        )
    )
    far = lax.ppermute(far, "gz", straight)
    near = lax.ppermute(near, "gz", crossing)
    partner = swap(partner)
    block = (FOLDS, LANES)
    folded, to_down, to_up = call(
        fold_kernel,
        "fold",
        [(22 * ROWS * FOLDS, LANES), (SIDE, *block), (SIDE, *block)],
        [design, partner, near, far],
    )
    height, to_down, to_up = call(
        functools.partial(filter_kernel, chips, tiles),
        "filter",
        [(LAYERS, ROWS, *block), (MARGIN, 640), (MARGIN, 640)],
        [folded.reshape(22, ROWS, *block), from_up(to_down), from_down(to_up)],
        scratch=[(22, ROWS + 2 * REACH, *block)] * 3 + [(MARGIN * FOLDS, LANES)],
    )

    def widen(rows, edge, name):
        (out,) = call(functools.partial(widen_kernel, edge), name, [(MARGIN * FOLDS, LANES)], [rows])
        return out.reshape(MARGIN, *block)

    height_up = widen(from_up(to_down), 0, "widen_up")
    height_down = widen(from_down(to_up), tiles - 1, "widen_down")

    def spread(folded, scale, name):
        own, other = call(
            functools.partial(unfold_kernel, scale),
            name,
            [(8, ROWS, 512), (8, ROWS, 512)],
            [folded.reshape(LAYERS * ROWS * FOLDS, LANES)],
        )
        return own, swap(other)

    def assemble(own, other):
        return jnp.where(
            core == 0, jnp.concatenate([own, other], axis=2), jnp.concatenate([other, own], axis=2)
        )

    shown, height_up = lax.optimization_barrier((height, height_up))
    shown = spread(shown, 1.0 / HALF, "blueprint")
    height, shown = lax.optimization_barrier((height, shown))
    printed = jnp.zeros((LAYERS, ROWS, *block), jnp.float32)
    received = []
    for turn in range(chips):
        operands = [*received, height, height_up, height_down, printed]
        printed, *top = call(
            functools.partial(chain_kernel, turn, tiles),
            "chain",
            [(LAYERS, ROWS, *block), (ROWS, *block)][: 2 if turn < chips - 1 else 1],
            operands,
            scratch=[(48, *block)] * 2,
            aliases={len(operands) - 1: 0},
        )
        if turn < chips - 1:
            received = [
                lax.ppermute(
                    top[0],
                    AXES,
                    [
                        (at(2 * turn + c, t), at(2 * turn + 2 + c, t + away))
                        for c in range(2)
                        for t in range(tiles)
                        if 0 <= t + away < tiles
                    ],
                )
                for away in (1, -1, 0)
            ]
        if turn == 0:
            printed, blueprint = lax.optimization_barrier((printed, assemble(*shown)))
    return blueprint, assemble(*spread(printed, 0.5 / HALF, "printed"))


def solution(mesh):
    spec = P("gz", "xy", None)
    return jax.shard_map(local, mesh=mesh, in_specs=(spec,), out_specs=(spec, spec), check_vma=False)
```

```python
import functools
import math

import jax
import jax.numpy as jnp
from jax import lax
from jax.experimental import pallas as pl
from jax.experimental.pallas import tpu as pltpu
from jax.sharding import PartitionSpec as P

LAYERS = 16
ROWS = 16
FOLDS = 8
LANES = 128
STRIDE = 80
HALO = 24
REACH = 3
PART = 768
AXES = ("gz", "xy")

FILTER_R2 = 4.0
PROJ_BETA = 8.0
PROJ_ETA = 0.5
SHARPNESS = 16.0
SMOOTH_EPS = 0.0001
HALF = 0.5 * SHARPNESS / math.log(2.0)
OUTSIDE = -50.0
TINY = 2.0**-100
MARGIN_AT = [sum(15 - j for j in range(k)) for k in range(16)]
MARGIN = MARGIN_AT[15]
SIDE = 20 + 18 + 16


def place():
    slab = lax.axis_index("gz")
    return lax.div(slab, 2), lax.rem(slab, 2), lax.axis_index("xy")


def lane_of(shape=(FOLDS, LANES)):
    return lax.broadcasted_iota(jnp.int32, shape, len(shape) - 1)


def column_mask(core):
    fold = lax.broadcasted_iota(jnp.int32, (FOLDS, LANES), 0)
    column = 384 * core + STRIDE * fold + lane_of() - HALO
    return (column >= 0) & (column < 1024)


def fold_rows(tiles, lane, store):
    for s in range(FOLDS):
        a, shift = divmod(LANES - HALO + STRIDE * s, LANES)
        block = tiles[a]
        if shift:
            first = pltpu.roll(tiles[a], LANES - shift, 1)
            second = pltpu.roll(tiles[a + 1], LANES - shift, 1)
            block = jnp.where(lane < LANES - shift, first, second)
        store(s, block)


def unfold_rows(blocks, lane):
    tiles = []
    for a in range(5):
        tile = None
        for s in range(FOLDS):
            low = max(LANES * a, STRIDE * s)
            if low >= min(LANES * a + LANES, STRIDE * s + STRIDE):
                continue
            piece = pltpu.roll(blocks[s], (STRIDE * s - LANES * a - HALO) % LANES, 1)
            tile = piece if tile is None else jnp.where(lane >= low - LANES * a, piece, tile)
        tiles.append(tile)
    return tiles


def fold_kernel(own, partner, near, far, out, to_down, to_up):
    unused, core, unused = place()
    lane = lane_of()

    def fold(source, start, base, count):
        def layer(i, carry):
            for group in range(2):
                tiles = []
                for a in range(7):
                    at = jnp.clip(a - 1 + core, 0, 5) * LANES + start
                    tile = source[i, pl.ds(8 * group, 8), pl.ds(pl.multiple_of(at, LANES), LANES)]
                    if a == 0:
                        tile = jnp.where(core == 0, 0.0, tile)
                    if a == 6:
                        tile = jnp.where(core == 1, 0.0, tile)
                    tiles.append(tile)
                row = ((base + i) * ROWS + 8 * group) * FOLDS

                def store(s, block):
                    out[pl.ds(row + s, 8, stride=FOLDS), :] = block

                fold_rows(tiles, lane, store)
            return carry

        lax.fori_loop(0, count, layer, 0, unroll=count)

    fold(own, 256 * core, REACH + 8 * core, 8)
    fold(partner, 0, REACH + 8 * (1 - core), 8)
    fold(near, 0, 19 * core, REACH)
    fold(far, 0, 19 * (1 - core), REACH)
    at = 0
    for away in range(REACH):
        for i in range(1 + away, 21 - away):
            to_down[at] = out[pl.ds((i * ROWS + 15 - away) * FOLDS, FOLDS), :]
            to_up[at] = out[pl.ds((i * ROWS + away) * FOLDS, FOLDS), :]
            at += 1


def filter_kernel(count_chips, count_tiles, own, up, down, height, to_down, to_up, cells, first, second, packed):
    chip, core, tile = place()
    inside = column_mask(core)
    scale = jnp.where(inside, 1.0 / (1.0 + 6.0 * FILTER_R2), 0.0)
    above = jnp.where(tile > 0, 1.0, 0.0)
    below = jnp.where(tile < count_tiles - 1, 1.0, 0.0)

    def gather(i, carry):
        cells[i, pl.ds(REACH, ROWS)] = own[i]
        return carry

    lax.fori_loop(0, 22, gather, 0, unroll=22)
    at = 0
    for away in range(REACH):
        for i in range(1 + away, 21 - away):
            cells[i, REACH - 1 - away] = up[at]
            cells[i, REACH + ROWS + away] = down[at]
            at += 1

    def sweep(source, step, store):
        rim = REACH - step

        def layer(i, rows):
            held = jnp.where(((chip == 0) & (i < REACH)) | ((chip == count_chips - 1) & (i >= REACH + LAYERS)), 0.0, scale)
            for r in rows:
                middle = source[i, r]
                total = source[i - 1, r] + source[i + 1, r] + source[i, r - 1] + source[i, r + 1]
                total = total + pltpu.roll(middle, 1, 1) + pltpu.roll(middle, LANES - 1, 1)
                factor = held
                if r < REACH:
                    factor = held * above
                if r >= REACH + ROWS:
                    factor = held * below
                store(i, r, (cells[i, r] + FILTER_R2 * total) * factor)

        def body(i, carry):
            layer(i, range(REACH - rim, REACH + ROWS + rim))
            return carry

        for away in range(rim):
            for i in (REACH - rim + away, REACH + LAYERS + rim - 1 - away):
                layer(i, range(REACH - away, REACH + ROWS + away))
        lax.fori_loop(REACH, REACH + LAYERS, body, 0, unroll=LAYERS)

    def keep(target):
        def store(i, r, value):
            target[i, r] = value

        return store

    base = math.tanh(PROJ_BETA * PROJ_ETA)
    gain = HALF / (math.tanh(PROJ_BETA * PROJ_ETA) + math.tanh(PROJ_BETA * (1.0 - PROJ_ETA)))

    def project(i, r, field):
        value = gain * (base + jnp.tanh(PROJ_BETA * field - PROJ_BETA * PROJ_ETA))
        height[i - REACH, r - REACH] = jnp.where(inside, value, OUTSIDE)

    sweep(cells, 1, keep(first))
    sweep(first, 2, keep(second))
    sweep(second, 3, project)
    lane = lane_of()
    for target, low in ((to_down, 1), (to_up, 0)):
        for k in range(15):
            rows = height[k, pl.ds(low * (k + 1), 15 - k)]
            packed[pl.ds(MARGIN_AT[k] * FOLDS, (15 - k) * FOLDS), :] = rows.reshape((15 - k) * FOLDS, LANES)
        for group in range(MARGIN // 8):
            blocks = [packed[pl.ds(8 * group * FOLDS + s, 8, stride=FOLDS), :] for s in range(FOLDS)]
            for a, tile in enumerate(unfold_rows(blocks, lane)):
                target[pl.ds(8 * group, 8), pl.ds(LANES * a, LANES)] = tile


def widen_kernel(edge, rows, out):
    unused, core, tile = place()
    lane = lane_of()
    zero = jnp.zeros((8, LANES), jnp.float32)
    for group in range(MARGIN // 8):
        tiles = [rows[pl.ds(8 * group, 8), pl.ds(LANES * a, LANES)] for a in range(5)]

        def store(s, block):
            out[pl.ds(8 * group * FOLDS + s, 8, stride=FOLDS), :] = block

        fold_rows([zero, *tiles, zero], lane, store)
    inside = column_mask(core) & (tile != edge)
    for r in range(MARGIN):
        at = pl.ds(r * FOLDS, FOLDS)
        out[at, :] = jnp.where(inside, out[at, :], OUTSIDE)


def chain_kernel(turn, count_tiles, *refs):
    received, refs = (refs[:3], refs[3:]) if turn else ((), refs)
    height, height_up, height_down, unused, printed, *top, even, odd = refs
    chip, core, tile = place()

    @pl.when(chip == turn)
    def run():
        inside = column_mask(core)
        lane = lane_of()
        if turn:
            middle, up, down = received
            for r in range(ROWS):
                even[r] = up[r] + TINY
                even[ROWS + r] = middle[r] + TINY
                even[2 * ROWS + r] = down[r] + TINY
        else:
            ones = jnp.where(inside, math.exp(SHARPNESS), TINY)
            ones_up = jnp.where(tile > 0, ones, TINY)
            ones_down = jnp.where(tile < count_tiles - 1, ones, TINY)
            for r in range(ROWS):
                even[r] = ones_up
                even[ROWS + r] = ones
                even[2 * ROWS + r] = ones_down
        level = HALF * math.sqrt(SMOOTH_EPS)
        for k in range(LAYERS):
            source, target = (even, odd) if k % 2 == 0 else (odd, even)
            for j in range(k + 1, 47 - k):
                total = source[j - 1] + source[j] + source[j + 1]
                total = total + pltpu.roll(total, 1, 1) + pltpu.roll(total, LANES - 1, 1)
                support = jnp.log(total) * (0.5 / math.log(2.0)) - 0.5 * math.log2(9.0)
                if j < ROWS:
                    blue = height_up[MARGIN_AT[k] + j - 1 - k]
                elif j < 2 * ROWS:
                    blue = height[k, j - ROWS]
                else:
                    blue = height_down[MARGIN_AT[k] + j - 2 * ROWS]
                gap = blue - support
                square = gap * gap + level * level
                value = (blue + support + level) - square * lax.rsqrt(square)
                weight = jnp.exp2(value)
                if ROWS <= j < 2 * ROWS:
                    printed[k, j - ROWS] = value
                if k < LAYERS - 1:
                    target[j] = weight
                elif top:
                    before = pltpu.roll(pltpu.roll(weight, 1, 0), LANES - STRIDE, 1)
                    after = pltpu.roll(pltpu.roll(weight, FOLDS - 1, 0), STRIDE, 1)
                    weight = jnp.where(lane < HALO, before, weight)
                    weight = jnp.where(lane >= HALO + STRIDE, after, weight)
                    top[0][j - ROWS] = jnp.where(inside, weight, 0.0)


def unfold_kernel(scale, folded, own, partner):
    unused, core, unused = place()
    lane = lane_of()

    def unfold(target, base):
        def layer(i, carry):
            for group in range(2):
                row = ((base + i) * ROWS + 8 * group) * FOLDS
                blocks = [folded[pl.ds(row + s, 8, stride=FOLDS), :] * scale for s in range(FOLDS)]
                tiles = unfold_rows(blocks, lane)
                for a in range(4):
                    target[i, pl.ds(8 * group, 8), pl.ds(LANES * a, LANES)] = jnp.where(core == 0, tiles[a], tiles[a + 1])
            return carry

        lax.fori_loop(0, 8, layer, 0, unroll=8)

    unfold(own, 8 * core)
    unfold(partner, 8 * (1 - core))


def call(kernel, name, outs, operands, scratch=(), aliases=None):
    held = [pltpu.with_memory_space_constraint(x, pltpu.VMEM) for x in operands]
    vmem = pl.BlockSpec(memory_space=pltpu.VMEM)
    return pl.pallas_call(
        kernel,
        name=name,
        out_shape=[pltpu.VMEM(shape, jnp.float32) for shape in outs],
        in_specs=[vmem] * len(held),
        out_specs=[vmem] * len(outs),
        scratch_shapes=[pltpu.VMEM(shape, jnp.float32) for shape in scratch],
        input_output_aliases=aliases or {},
        compiler_params=pltpu.CompilerParams(vmem_limit_bytes=24 * 1024 * 1024),
    )(*held)


def local(design):
    slabs = lax.axis_size("gz")
    tiles = lax.axis_size("xy")
    chips = slabs // 2
    unused, core, unused = place()

    def at(slab, tile):
        return slab * tiles + tile

    def swap(block):
        return lax.ppermute(block, "gz", [(i, i ^ 1) for i in range(slabs)])

    def from_up(block):
        return lax.ppermute(block, "xy", [(i, i + 1) for i in range(tiles - 1)])

    def from_down(block):
        return lax.ppermute(block, "xy", [(i + 1, i) for i in range(tiles - 1)])

    rim = jnp.where(core == 0, design[:REACH], design[8 - REACH :])
    left, right = design[:, :, :PART], design[:, :, 1024 - PART :]
    rim_left, rim_right = rim[:, :, :PART], rim[:, :, 1024 - PART :]
    crossing = [(i, j) for k in range(1, chips) for i, j in ((2 * k - 1, 2 * k), (2 * k, 2 * k - 1))]
    straight = [(i, j) for k in range(1, chips) for i, j in ((2 * k - 1, 2 * k + 1), (2 * k, 2 * k - 2))]
    partner = swap(jnp.where(core == 0, right, left))
    near = lax.ppermute(jnp.where(core == 0, rim_right, rim_left), "gz", crossing)
    far = lax.ppermute(jnp.where(core == 0, rim_left, rim_right), "gz", straight)
    block = (FOLDS, LANES)
    folded, to_down, to_up = call(
        fold_kernel,
        "fold",
        [(22 * ROWS * FOLDS, LANES), (SIDE, *block), (SIDE, *block)],
        [design, partner, near, far],
    )
    height, to_down, to_up = call(
        functools.partial(filter_kernel, chips, tiles),
        "filter",
        [(LAYERS, ROWS, *block), (MARGIN, 640), (MARGIN, 640)],
        [folded.reshape(22, ROWS, *block), from_up(to_down), from_down(to_up)],
        scratch=[(22, ROWS + 2 * REACH, *block)] * 3 + [(MARGIN * FOLDS, LANES)],
    )

    def widen(rows, edge, name):
        (out,) = call(functools.partial(widen_kernel, edge), name, [(MARGIN * FOLDS, LANES)], [rows])
        return out.reshape(MARGIN, *block)

    height_up = widen(from_up(to_down), 0, "widen_up")
    height_down = widen(from_down(to_up), tiles - 1, "widen_down")

    def spread(folded, scale, name):
        own, other = call(
            functools.partial(unfold_kernel, scale),
            name,
            [(8, ROWS, 512), (8, ROWS, 512)],
            [folded.reshape(LAYERS * ROWS * FOLDS, LANES)],
        )
        return own, swap(other)

    def assemble(own, other):
        return jnp.where(
            core == 0, jnp.concatenate([own, other], axis=2), jnp.concatenate([other, own], axis=2)
        )

    shown, height_up = lax.optimization_barrier((height, height_up))
    shown = spread(shown, 1.0 / HALF, "blueprint")
    height, shown = lax.optimization_barrier((height, shown))
    printed = jnp.zeros((LAYERS, ROWS, *block), jnp.float32)
    received = []
    for turn in range(chips):
        operands = [*received, height, height_up, height_down, printed]
        printed, *top = call(
            functools.partial(chain_kernel, turn, tiles),
            "chain",
            [(LAYERS, ROWS, *block), (ROWS, *block)][: 2 if turn < chips - 1 else 1],
            operands,
            scratch=[(48, *block)] * 2,
            aliases={len(operands) - 1: 0},
        )
        if turn < chips - 1:
            received = [
                lax.ppermute(
                    top[0],
                    AXES,
                    [
                        (at(2 * turn + c, t), at(2 * turn + 2 + c, t + away))
                        for c in range(2)
                        for t in range(tiles)
                        if 0 <= t + away < tiles
                    ],
                )
                for away in (0, 1, -1)
            ]
        if turn == 0:
            printed, blueprint = lax.optimization_barrier((printed, assemble(*shown)))
    return blueprint, assemble(*spread(printed, 0.5 / HALF, "printed"))


def solution(mesh):
    spec = P("gz", "xy", None)
    return jax.shard_map(local, mesh=mesh, in_specs=(spec,), out_specs=(spec, spec), check_vma=False)
```

```python
import functools
import math

import jax
import jax.numpy as jnp
from jax import lax
from jax.experimental import pallas as pl
from jax.experimental.pallas import tpu as pltpu
from jax.sharding import PartitionSpec as P

LAYERS = 16
ROWS = 16
FOLDS = 8
LANES = 128
STRIDE = 80
HALO = 24
REACH = 3
PART = 768
AXES = ("gz", "xy")

FILTER_R2 = 4.0
PROJ_BETA = 8.0
PROJ_ETA = 0.5
SHARPNESS = 16.0
SMOOTH_EPS = 0.0001
HALF = 0.5 * SHARPNESS / math.log(2.0)
OUTSIDE = -50.0
TINY = 2.0**-100
MARGIN_AT = [sum(15 - j for j in range(k)) for k in range(16)]
MARGIN = MARGIN_AT[15]
SIDE = 20 + 18 + 16


def place():
    slab = lax.axis_index("gz")
    return lax.div(slab, 2), lax.rem(slab, 2), lax.axis_index("xy")


def lane_of(shape=(FOLDS, LANES)):
    return lax.broadcasted_iota(jnp.int32, shape, len(shape) - 1)


def column_mask(core):
    fold = lax.broadcasted_iota(jnp.int32, (FOLDS, LANES), 0)
    column = 384 * core + STRIDE * fold + lane_of() - HALO
    return (column >= 0) & (column < 1024)


def fetch_kernel(design, own, partner, near, far, done):
    unused, core, unused = place()
    here = pl.ds(pl.multiple_of(256 * core, LANES), PART)
    there = pl.ds(pl.multiple_of(256 * (1 - core), LANES), PART)
    rim = pl.ds((8 - REACH) * core, REACH)
    copies = [
        pltpu.make_async_copy(design.at[rim, :, here], far, done.at[0]),
        pltpu.make_async_copy(design.at[rim, :, there], near, done.at[1]),
        pltpu.make_async_copy(design.at[:, :, there], partner, done.at[2]),
        pltpu.make_async_copy(design.at[:, :, here], own, done.at[3]),
    ]
    for copy in copies:
        copy.start()
    for copy in copies:
        copy.wait()


def fold_rows(tiles, lane, store):
    for s in range(FOLDS):
        a, shift = divmod(LANES - HALO + STRIDE * s, LANES)
        block = tiles[a]
        if shift:
            first = pltpu.roll(tiles[a], LANES - shift, 1)
            second = pltpu.roll(tiles[a + 1], LANES - shift, 1)
            block = jnp.where(lane < LANES - shift, first, second)
        store(s, block)


def unfold_rows(blocks, lane):
    tiles = []
    for a in range(5):
        tile = None
        for s in range(FOLDS):
            low = max(LANES * a, STRIDE * s)
            if low >= min(LANES * a + LANES, STRIDE * s + STRIDE):
                continue
            piece = pltpu.roll(blocks[s], (STRIDE * s - LANES * a - HALO) % LANES, 1)
            tile = piece if tile is None else jnp.where(lane >= low - LANES * a, piece, tile)
        tiles.append(tile)
    return tiles


def fold_kernel(own, partner, near, far, out, to_down, to_up):
    unused, core, unused = place()
    lane = lane_of()

    def fold(source, base, count):
        def layer(i, carry):
            for group in range(2):
                tiles = []
                for a in range(7):
                    at = jnp.clip(a - 1 + core, 0, 5) * LANES
                    tile = source[i, pl.ds(8 * group, 8), pl.ds(pl.multiple_of(at, LANES), LANES)]
                    if a == 0:
                        tile = jnp.where(core == 0, 0.0, tile)
                    if a == 6:
                        tile = jnp.where(core == 1, 0.0, tile)
                    tiles.append(tile)
                row = ((base + i) * ROWS + 8 * group) * FOLDS

                def store(s, block):
                    out[pl.ds(row + s, 8, stride=FOLDS), :] = block

                fold_rows(tiles, lane, store)
            return carry

        lax.fori_loop(0, count, layer, 0, unroll=count)

    fold(own, REACH + 8 * core, 8)
    fold(partner, REACH + 8 * (1 - core), 8)
    fold(near, 19 * core, REACH)
    fold(far, 19 * (1 - core), REACH)
    at = 0
    for away in range(REACH):
        for i in range(1 + away, 21 - away):
            to_down[at] = out[pl.ds((i * ROWS + 15 - away) * FOLDS, FOLDS), :]
            to_up[at] = out[pl.ds((i * ROWS + away) * FOLDS, FOLDS), :]
            at += 1


def filter_kernel(count_chips, count_tiles, own, up, down, height, to_down, to_up, cells, first, second, packed):
    chip, core, tile = place()
    inside = column_mask(core)
    scale = jnp.where(inside, 1.0 / (1.0 + 6.0 * FILTER_R2), 0.0)
    above = jnp.where(tile > 0, 1.0, 0.0)
    below = jnp.where(tile < count_tiles - 1, 1.0, 0.0)

    def gather(i, carry):
        cells[i, pl.ds(REACH, ROWS)] = own[i]
        return carry

    lax.fori_loop(0, 22, gather, 0, unroll=22)
    at = 0
    for away in range(REACH):
        for i in range(1 + away, 21 - away):
            cells[i, REACH - 1 - away] = up[at]
            cells[i, REACH + ROWS + away] = down[at]
            at += 1

    def sweep(source, step, store):
        rim = REACH - step

        def layer(i, rows):
            held = jnp.where(((chip == 0) & (i < REACH)) | ((chip == count_chips - 1) & (i >= REACH + LAYERS)), 0.0, scale)
            for r in rows:
                middle = source[i, r]
                total = source[i - 1, r] + source[i + 1, r] + source[i, r - 1] + source[i, r + 1]
                total = total + pltpu.roll(middle, 1, 1) + pltpu.roll(middle, LANES - 1, 1)
                factor = held
                if r < REACH:
                    factor = held * above
                if r >= REACH + ROWS:
                    factor = held * below
                store(i, r, (cells[i, r] + FILTER_R2 * total) * factor)

        def body(i, carry):
            layer(i, range(REACH - rim, REACH + ROWS + rim))
            return carry

        for away in range(rim):
            for i in (REACH - rim + away, REACH + LAYERS + rim - 1 - away):
                layer(i, range(REACH - away, REACH + ROWS + away))
        lax.fori_loop(REACH, REACH + LAYERS, body, 0, unroll=LAYERS)

    def keep(target):
        def store(i, r, value):
            target[i, r] = value

        return store

    base = math.tanh(PROJ_BETA * PROJ_ETA)
    gain = HALF / (math.tanh(PROJ_BETA * PROJ_ETA) + math.tanh(PROJ_BETA * (1.0 - PROJ_ETA)))

    def project(i, r, field):
        value = gain * (base + jnp.tanh(PROJ_BETA * field - PROJ_BETA * PROJ_ETA))
        height[i - REACH, r - REACH] = jnp.where(inside, value, OUTSIDE)

    sweep(cells, 1, keep(first))
    sweep(first, 2, keep(second))
    sweep(second, 3, project)
    lane = lane_of()
    for target, low in ((to_down, 1), (to_up, 0)):
        for k in range(15):
            rows = height[k, pl.ds(low * (k + 1), 15 - k)]
            packed[pl.ds(MARGIN_AT[k] * FOLDS, (15 - k) * FOLDS), :] = rows.reshape((15 - k) * FOLDS, LANES)
        for group in range(MARGIN // 8):
            blocks = [packed[pl.ds(8 * group * FOLDS + s, 8, stride=FOLDS), :] for s in range(FOLDS)]
            for a, tile in enumerate(unfold_rows(blocks, lane)):
                target[pl.ds(8 * group, 8), pl.ds(LANES * a, LANES)] = tile


def widen_kernel(edge, rows, out):
    unused, core, tile = place()
    lane = lane_of()
    zero = jnp.zeros((8, LANES), jnp.float32)
    for group in range(MARGIN // 8):
        tiles = [rows[pl.ds(8 * group, 8), pl.ds(LANES * a, LANES)] for a in range(5)]

        def store(s, block):
            out[pl.ds(8 * group * FOLDS + s, 8, stride=FOLDS), :] = block

        fold_rows([zero, *tiles, zero], lane, store)
    inside = column_mask(core) & (tile != edge)
    for r in range(MARGIN):
        at = pl.ds(r * FOLDS, FOLDS)
        out[at, :] = jnp.where(inside, out[at, :], OUTSIDE)


def chain_kernel(turn, count_tiles, *refs):
    received, refs = (refs[:3], refs[3:]) if turn else ((), refs)
    height, height_up, height_down, unused, printed, *top, even, odd = refs
    chip, core, tile = place()

    @pl.when(chip == turn)
    def run():
        inside = column_mask(core)
        lane = lane_of()
        if turn:
            middle, up, down = received
            for r in range(ROWS):
                even[r] = up[r] + TINY
                even[ROWS + r] = middle[r] + TINY
                even[2 * ROWS + r] = down[r] + TINY
        else:
            ones = jnp.where(inside, math.exp(SHARPNESS), TINY)
            ones_up = jnp.where(tile > 0, ones, TINY)
            ones_down = jnp.where(tile < count_tiles - 1, ones, TINY)
            for r in range(ROWS):
                even[r] = ones_up
                even[ROWS + r] = ones
                even[2 * ROWS + r] = ones_down
        level = HALF * math.sqrt(SMOOTH_EPS)
        for k in range(LAYERS):
            source, target = (even, odd) if k % 2 == 0 else (odd, even)
            for j in range(k + 1, 47 - k):
                total = source[j - 1] + source[j] + source[j + 1]
                total = total + pltpu.roll(total, 1, 1) + pltpu.roll(total, LANES - 1, 1)
                support = jnp.log(total) * (0.5 / math.log(2.0)) - 0.5 * math.log2(9.0)
                if j < ROWS:
                    blue = height_up[MARGIN_AT[k] + j - 1 - k]
                elif j < 2 * ROWS:
                    blue = height[k, j - ROWS]
                else:
                    blue = height_down[MARGIN_AT[k] + j - 2 * ROWS]
                gap = blue - support
                square = gap * gap + level * level
                value = (blue + support + level) - square * lax.rsqrt(square)
                weight = jnp.exp2(value)
                if ROWS <= j < 2 * ROWS:
                    printed[k, j - ROWS] = value
                if k < LAYERS - 1:
                    target[j] = weight
                elif top:
                    before = pltpu.roll(pltpu.roll(weight, 1, 0), LANES - STRIDE, 1)
                    after = pltpu.roll(pltpu.roll(weight, FOLDS - 1, 0), STRIDE, 1)
                    weight = jnp.where(lane < HALO, before, weight)
                    weight = jnp.where(lane >= HALO + STRIDE, after, weight)
                    top[0][j - ROWS] = jnp.where(inside, weight, 0.0)


def unfold_kernel(scale, folded, own, partner):
    unused, core, unused = place()
    lane = lane_of()

    def unfold(target, base):
        def layer(i, carry):
            for group in range(2):
                row = ((base + i) * ROWS + 8 * group) * FOLDS
                blocks = [folded[pl.ds(row + s, 8, stride=FOLDS), :] * scale for s in range(FOLDS)]
                tiles = unfold_rows(blocks, lane)
                for a in range(4):
                    target[i, pl.ds(8 * group, 8), pl.ds(LANES * a, LANES)] = jnp.where(core == 0, tiles[a], tiles[a + 1])
            return carry

        lax.fori_loop(0, 8, layer, 0, unroll=8)

    unfold(own, 8 * core)
    unfold(partner, 8 * (1 - core))


def call(kernel, name, outs, operands, scratch=(), aliases=None):
    held = [pltpu.with_memory_space_constraint(x, pltpu.VMEM) for x in operands]
    vmem = pl.BlockSpec(memory_space=pltpu.VMEM)
    return pl.pallas_call(
        kernel,
        name=name,
        out_shape=[pltpu.VMEM(shape, jnp.float32) for shape in outs],
        in_specs=[vmem] * len(held),
        out_specs=[vmem] * len(outs),
        scratch_shapes=[pltpu.VMEM(shape, jnp.float32) for shape in scratch],
        input_output_aliases=aliases or {},
        compiler_params=pltpu.CompilerParams(vmem_limit_bytes=24 * 1024 * 1024),
    )(*held)


def local(design):
    slabs = lax.axis_size("gz")
    tiles = lax.axis_size("xy")
    chips = slabs // 2
    unused, core, unused = place()

    def at(slab, tile):
        return slab * tiles + tile

    def swap(block):
        return lax.ppermute(block, "gz", [(i, i ^ 1) for i in range(slabs)])

    def from_up(block):
        return lax.ppermute(block, "xy", [(i, i + 1) for i in range(tiles - 1)])

    def from_down(block):
        return lax.ppermute(block, "xy", [(i + 1, i) for i in range(tiles - 1)])

    crossing = [(i, j) for k in range(1, chips) for i, j in ((2 * k - 1, 2 * k), (2 * k, 2 * k - 1))]
    straight = [(i, j) for k in range(1, chips) for i, j in ((2 * k - 1, 2 * k + 1), (2 * k, 2 * k - 2))]
    vmem = pl.BlockSpec(memory_space=pltpu.VMEM)
    whole, rim = (8, ROWS, PART), (REACH, ROWS, PART)
    own, partner, near, far = pl.pallas_call(
        fetch_kernel,
        name="fetch",
        out_shape=[pltpu.VMEM(shape, jnp.float32) for shape in (whole, whole, rim, rim)],
        in_specs=[pl.BlockSpec(memory_space=pltpu.HBM)],
        out_specs=[vmem] * 4,
        scratch_shapes=[pltpu.SemaphoreType.DMA((4,))],
    )(pltpu.with_memory_space_constraint(design, pltpu.HBM))
    far = lax.ppermute(far, "gz", straight)
    near = lax.ppermute(near, "gz", crossing)
    partner = swap(partner)
    block = (FOLDS, LANES)
    folded, to_down, to_up = call(
        fold_kernel,
        "fold",
        [(22 * ROWS * FOLDS, LANES), (SIDE, *block), (SIDE, *block)],
        [own, partner, near, far],
    )
    height, to_down, to_up = call(
        functools.partial(filter_kernel, chips, tiles),
        "filter",
        [(LAYERS, ROWS, *block), (MARGIN, 640), (MARGIN, 640)],
        [folded.reshape(22, ROWS, *block), from_up(to_down), from_down(to_up)],
        scratch=[(22, ROWS + 2 * REACH, *block)] * 3 + [(MARGIN * FOLDS, LANES)],
    )

    def widen(rows, edge, name):
        (out,) = call(functools.partial(widen_kernel, edge), name, [(MARGIN * FOLDS, LANES)], [rows])
        return out.reshape(MARGIN, *block)

    height_up = widen(from_up(to_down), 0, "widen_up")
    height_down = widen(from_down(to_up), tiles - 1, "widen_down")

    def spread(folded, scale, name):
        own, other = call(
            functools.partial(unfold_kernel, scale),
            name,
            [(8, ROWS, 512), (8, ROWS, 512)],
            [folded.reshape(LAYERS * ROWS * FOLDS, LANES)],
        )
        return own, swap(other)

    def assemble(own, other):
        return jnp.where(
            core == 0, jnp.concatenate([own, other], axis=2), jnp.concatenate([other, own], axis=2)
        )

    shown = spread(height, 1.0 / HALF, "blueprint")
    height, shown = lax.optimization_barrier((height, shown))
    printed = jnp.zeros((LAYERS, ROWS, *block), jnp.float32)
    received = []
    for turn in range(chips):
        operands = [*received, height, height_up, height_down, printed]
        printed, *top = call(
            functools.partial(chain_kernel, turn, tiles),
            "chain",
            [(LAYERS, ROWS, *block), (ROWS, *block)][: 2 if turn < chips - 1 else 1],
            operands,
            scratch=[(48, *block)] * 2,
            aliases={len(operands) - 1: 0},
        )
        if turn < chips - 1:
            received = [
                lax.ppermute(
                    top[0],
                    AXES,
                    [
                        (at(2 * turn + c, t), at(2 * turn + 2 + c, t + away))
                        for c in range(2)
                        for t in range(tiles)
                        if 0 <= t + away < tiles
                    ],
                )
                for away in (0, 1, -1)
            ]
        if turn == 0:
            printed, blueprint = lax.optimization_barrier((printed, assemble(*shown)))
    return blueprint, assemble(*spread(printed, 0.5 / HALF, "printed"))


def solution(mesh):
    spec = P("gz", "xy", None)
    return jax.shard_map(local, mesh=mesh, in_specs=(spec,), out_specs=(spec, spec), check_vma=False)
```

```python
import functools
import math

import jax
import jax.numpy as jnp
from jax import lax
from jax.experimental import pallas as pl
from jax.experimental.pallas import tpu as pltpu
from jax.sharding import PartitionSpec as P

LAYERS = 16
ROWS = 16
FOLDS = 8
LANES = 128
STRIDE = 80
HALO = 24
REACH = 3
PART = 768
AXES = ("gz", "xy")

FILTER_R2 = 4.0
PROJ_BETA = 8.0
PROJ_ETA = 0.5
SHARPNESS = 16.0
SMOOTH_EPS = 0.0001
HALF = 0.5 * SHARPNESS / math.log(2.0)
OUTSIDE = -50.0
TINY = 2.0**-100
MARGIN_AT = [sum(15 - j for j in range(k)) for k in range(16)]
MARGIN = MARGIN_AT[15]
SIDE = 20 + 18 + 16


def place():
    slab = lax.axis_index("gz")
    return lax.div(slab, 2), lax.rem(slab, 2), lax.axis_index("xy")


def lane_of(shape=(FOLDS, LANES)):
    return lax.broadcasted_iota(jnp.int32, shape, len(shape) - 1)


def column_mask(core):
    fold = lax.broadcasted_iota(jnp.int32, (FOLDS, LANES), 0)
    column = 384 * core + STRIDE * fold + lane_of() - HALO
    return (column >= 0) & (column < 1024)


def fetch_kernel(design, own, partner, near, far, done):
    unused, core, unused = place()
    here = pl.ds(pl.multiple_of(256 * core, LANES), PART)
    there = pl.ds(pl.multiple_of(256 * (1 - core), LANES), PART)
    rim = pl.ds((8 - REACH) * core, REACH)
    copies = [
        pltpu.make_async_copy(design.at[rim, :, here], far, done.at[0]),
        pltpu.make_async_copy(design.at[rim, :, there], near, done.at[1]),
        pltpu.make_async_copy(design.at[:, :, there], partner, done.at[2]),
        pltpu.make_async_copy(design.at[:, :, here], own, done.at[3]),
    ]
    for copy in copies:
        copy.start()
    for copy in copies:
        copy.wait()


def fold_rows(tiles, lane, store):
    for s in range(FOLDS):
        a, shift = divmod(LANES - HALO + STRIDE * s, LANES)
        block = tiles[a]
        if shift:
            first = pltpu.roll(tiles[a], LANES - shift, 1)
            second = pltpu.roll(tiles[a + 1], LANES - shift, 1)
            block = jnp.where(lane < LANES - shift, first, second)
        store(s, block)


def unfold_rows(blocks, lane):
    tiles = []
    for a in range(5):
        tile = None
        for s in range(FOLDS):
            low = max(LANES * a, STRIDE * s)
            if low >= min(LANES * a + LANES, STRIDE * s + STRIDE):
                continue
            piece = pltpu.roll(blocks[s], (STRIDE * s - LANES * a - HALO) % LANES, 1)
            tile = piece if tile is None else jnp.where(lane >= low - LANES * a, piece, tile)
        tiles.append(tile)
    return tiles


def fold_kernel(own, partner, near, far, out, to_down, to_up):
    unused, core, unused = place()
    lane = lane_of()

    def fold(source, base, count):
        def layer(i, carry):
            for group in range(2):
                tiles = []
                for a in range(7):
                    at = jnp.clip(a - 1 + core, 0, 5) * LANES
                    tile = source[i, pl.ds(8 * group, 8), pl.ds(pl.multiple_of(at, LANES), LANES)]
                    if a == 0:
                        tile = jnp.where(core == 0, 0.0, tile)
                    if a == 6:
                        tile = jnp.where(core == 1, 0.0, tile)
                    tiles.append(tile)
                row = ((base + i) * ROWS + 8 * group) * FOLDS

                def store(s, block):
                    out[pl.ds(row + s, 8, stride=FOLDS), :] = block

                fold_rows(tiles, lane, store)
            return carry

        lax.fori_loop(0, count, layer, 0, unroll=count)

    fold(own, REACH + 8 * core, 8)
    fold(partner, REACH + 8 * (1 - core), 8)
    fold(near, 19 * core, REACH)
    fold(far, 19 * (1 - core), REACH)
    at = 0
    for away in range(REACH):
        for i in range(1 + away, 21 - away):
            to_down[at] = out[pl.ds((i * ROWS + 15 - away) * FOLDS, FOLDS), :]
            to_up[at] = out[pl.ds((i * ROWS + away) * FOLDS, FOLDS), :]
            at += 1


def filter_kernel(count_chips, count_tiles, own, up, down, height, to_down, to_up, cells, first, second, packed):
    chip, core, tile = place()
    inside = column_mask(core)
    scale = jnp.where(inside, 1.0 / (1.0 + 6.0 * FILTER_R2), 0.0)
    above = jnp.where(tile > 0, 1.0, 0.0)
    below = jnp.where(tile < count_tiles - 1, 1.0, 0.0)

    def gather(i, carry):
        cells[i, pl.ds(REACH, ROWS)] = own[i]
        return carry

    lax.fori_loop(0, 22, gather, 0, unroll=22)
    at = 0
    for away in range(REACH):
        for i in range(1 + away, 21 - away):
            cells[i, REACH - 1 - away] = up[at]
            cells[i, REACH + ROWS + away] = down[at]
            at += 1

    def sweep(source, step, store):
        rim = REACH - step

        def layer(i, rows):
            held = jnp.where(((chip == 0) & (i < REACH)) | ((chip == count_chips - 1) & (i >= REACH + LAYERS)), 0.0, scale)
            for r in rows:
                middle = source[i, r]
                total = source[i - 1, r] + source[i + 1, r] + source[i, r - 1] + source[i, r + 1]
                total = total + pltpu.roll(middle, 1, 1) + pltpu.roll(middle, LANES - 1, 1)
                factor = held
                if r < REACH:
                    factor = held * above
                if r >= REACH + ROWS:
                    factor = held * below
                store(i, r, (cells[i, r] + FILTER_R2 * total) * factor)

        def body(i, carry):
            layer(i, range(REACH - rim, REACH + ROWS + rim))
            return carry

        for away in range(rim):
            for i in (REACH - rim + away, REACH + LAYERS + rim - 1 - away):
                layer(i, range(REACH - away, REACH + ROWS + away))
        lax.fori_loop(REACH, REACH + LAYERS, body, 0, unroll=LAYERS)

    def keep(target):
        def store(i, r, value):
            target[i, r] = value

        return store

    base = math.tanh(PROJ_BETA * PROJ_ETA)
    gain = HALF / (math.tanh(PROJ_BETA * PROJ_ETA) + math.tanh(PROJ_BETA * (1.0 - PROJ_ETA)))

    def project(i, r, field):
        value = gain * (base + jnp.tanh(PROJ_BETA * field - PROJ_BETA * PROJ_ETA))
        height[i - REACH, r - REACH] = jnp.where(inside, value, OUTSIDE)

    sweep(cells, 1, keep(first))
    sweep(first, 2, keep(second))
    sweep(second, 3, project)
    lane = lane_of()
    for target, low in ((to_down, 1), (to_up, 0)):
        for k in range(15):
            rows = height[k, pl.ds(low * (k + 1), 15 - k)]
            packed[pl.ds(MARGIN_AT[k] * FOLDS, (15 - k) * FOLDS), :] = rows.reshape((15 - k) * FOLDS, LANES)
        for group in range(MARGIN // 8):
            blocks = [packed[pl.ds(8 * group * FOLDS + s, 8, stride=FOLDS), :] for s in range(FOLDS)]
            for a, tile in enumerate(unfold_rows(blocks, lane)):
                target[pl.ds(8 * group, 8), pl.ds(LANES * a, LANES)] = tile


def widen_kernel(edge, rows, out):
    unused, core, tile = place()
    lane = lane_of()
    zero = jnp.zeros((8, LANES), jnp.float32)
    for group in range(MARGIN // 8):
        tiles = [rows[pl.ds(8 * group, 8), pl.ds(LANES * a, LANES)] for a in range(5)]

        def store(s, block):
            out[pl.ds(8 * group * FOLDS + s, 8, stride=FOLDS), :] = block

        fold_rows([zero, *tiles, zero], lane, store)
    inside = column_mask(core) & (tile != edge)
    for r in range(MARGIN):
        at = pl.ds(r * FOLDS, FOLDS)
        out[at, :] = jnp.where(inside, out[at, :], OUTSIDE)


def chain_kernel(turn, count_tiles, *refs):
    received, refs = (refs[:3], refs[3:]) if turn else ((), refs)
    height, height_up, height_down, unused, printed, *top, even, odd = refs
    chip, core, tile = place()

    def row(j):
        return pl.ds(j * FOLDS, FOLDS)

    @pl.when(chip == turn)
    def run():
        inside = column_mask(core)
        lane = lane_of()
        if turn:
            middle, up, down = received
            zero = jnp.zeros((8, LANES), jnp.float32)
            for source, first in ((up, 0), (middle, ROWS), (down, 2 * ROWS)):
                for group in range(2):
                    tiles = [source[pl.ds(8 * group, 8), pl.ds(LANES * a, LANES)] for a in range(5)]

                    def store(s, block):
                        even[pl.ds((first + 8 * group) * FOLDS + s, 8, stride=FOLDS), :] = block + TINY

                    fold_rows([zero, *tiles, zero], lane, store)
        else:
            ones = jnp.where(inside, math.exp(SHARPNESS), TINY)
            ones_up = jnp.where(tile > 0, ones, TINY)
            ones_down = jnp.where(tile < count_tiles - 1, ones, TINY)
            for r in range(ROWS):
                even[row(r), :] = ones_up
                even[row(ROWS + r), :] = ones
                even[row(2 * ROWS + r), :] = ones_down
        level = HALF * math.sqrt(SMOOTH_EPS)
        for k in range(LAYERS):
            source, target = (even, odd) if k % 2 == 0 else (odd, even)
            for j in range(k + 1, 47 - k):
                total = source[row(j - 1), :] + source[row(j), :] + source[row(j + 1), :]
                total = total + pltpu.roll(total, 1, 1) + pltpu.roll(total, LANES - 1, 1)
                support = jnp.log(total) * (0.5 / math.log(2.0)) - 0.5 * math.log2(9.0)
                if j < ROWS:
                    blue = height_up[MARGIN_AT[k] + j - 1 - k]
                elif j < 2 * ROWS:
                    blue = height[k, j - ROWS]
                else:
                    blue = height_down[MARGIN_AT[k] + j - 2 * ROWS]
                gap = blue - support
                square = gap * gap + level * level
                value = (blue + support + level) - square * lax.rsqrt(square)
                weight = jnp.exp2(value)
                if ROWS <= j < 2 * ROWS:
                    printed[k, j - ROWS] = value
                if k < LAYERS - 1 or top:
                    target[row(j), :] = weight
        for group in range(2 if top else 0):
            first = (ROWS + 8 * group) * FOLDS
            blocks = [even[pl.ds(first + s, 8, stride=FOLDS), :] for s in range(FOLDS)]
            for a, piece in enumerate(unfold_rows(blocks, lane)):
                top[0][pl.ds(8 * group, 8), pl.ds(LANES * a, LANES)] = piece


def unfold_kernel(scale, folded, own, partner):
    unused, core, unused = place()
    lane = lane_of()

    def unfold(target, base):
        def layer(i, carry):
            for group in range(2):
                row = ((base + i) * ROWS + 8 * group) * FOLDS
                blocks = [folded[pl.ds(row + s, 8, stride=FOLDS), :] * scale for s in range(FOLDS)]
                tiles = unfold_rows(blocks, lane)
                for a in range(4):
                    target[i, pl.ds(8 * group, 8), pl.ds(LANES * a, LANES)] = jnp.where(core == 0, tiles[a], tiles[a + 1])
            return carry

        lax.fori_loop(0, 8, layer, 0, unroll=8)

    unfold(own, 8 * core)
    unfold(partner, 8 * (1 - core))


def call(kernel, name, outs, operands, scratch=(), aliases=None):
    held = [pltpu.with_memory_space_constraint(x, pltpu.VMEM) for x in operands]
    vmem = pl.BlockSpec(memory_space=pltpu.VMEM)
    return pl.pallas_call(
        kernel,
        name=name,
        out_shape=[pltpu.VMEM(shape, jnp.float32) for shape in outs],
        in_specs=[vmem] * len(held),
        out_specs=[vmem] * len(outs),
        scratch_shapes=[pltpu.VMEM(shape, jnp.float32) for shape in scratch],
        input_output_aliases=aliases or {},
        compiler_params=pltpu.CompilerParams(vmem_limit_bytes=24 * 1024 * 1024),
    )(*held)


def local(design):
    slabs = lax.axis_size("gz")
    tiles = lax.axis_size("xy")
    chips = slabs // 2
    unused, core, unused = place()

    def at(slab, tile):
        return slab * tiles + tile

    def swap(block):
        return lax.ppermute(block, "gz", [(i, i ^ 1) for i in range(slabs)])

    def from_up(block):
        return lax.ppermute(block, "xy", [(i, i + 1) for i in range(tiles - 1)])

    def from_down(block):
        return lax.ppermute(block, "xy", [(i + 1, i) for i in range(tiles - 1)])

    crossing = [(i, j) for k in range(1, chips) for i, j in ((2 * k - 1, 2 * k), (2 * k, 2 * k - 1))]
    straight = [(i, j) for k in range(1, chips) for i, j in ((2 * k - 1, 2 * k + 1), (2 * k, 2 * k - 2))]
    vmem = pl.BlockSpec(memory_space=pltpu.VMEM)
    whole, rim = (8, ROWS, PART), (REACH, ROWS, PART)
    own, partner, near, far = pl.pallas_call(
        fetch_kernel,
        name="fetch",
        out_shape=[pltpu.VMEM(shape, jnp.float32) for shape in (whole, whole, rim, rim)],
        in_specs=[pl.BlockSpec(memory_space=pltpu.HBM)],
        out_specs=[vmem] * 4,
        scratch_shapes=[pltpu.SemaphoreType.DMA((4,))],
    )(pltpu.with_memory_space_constraint(design, pltpu.HBM))
    far = lax.ppermute(far, "gz", straight)
    near = lax.ppermute(near, "gz", crossing)
    partner = swap(partner)
    block = (FOLDS, LANES)
    folded, to_down, to_up = call(
        fold_kernel,
        "fold",
        [(22 * ROWS * FOLDS, LANES), (SIDE, *block), (SIDE, *block)],
        [own, partner, near, far],
    )
    height, to_down, to_up = call(
        functools.partial(filter_kernel, chips, tiles),
        "filter",
        [(LAYERS, ROWS, *block), (MARGIN, 640), (MARGIN, 640)],
        [folded.reshape(22, ROWS, *block), from_up(to_down), from_down(to_up)],
        scratch=[(22, ROWS + 2 * REACH, *block)] * 3 + [(MARGIN * FOLDS, LANES)],
    )

    def widen(rows, edge, name):
        (out,) = call(functools.partial(widen_kernel, edge), name, [(MARGIN * FOLDS, LANES)], [rows])
        return out.reshape(MARGIN, *block)

    height_up = widen(from_up(to_down), 0, "widen_up")
    height_down = widen(from_down(to_up), tiles - 1, "widen_down")

    def spread(folded, scale, name):
        own, other = call(
            functools.partial(unfold_kernel, scale),
            name,
            [(8, ROWS, 512), (8, ROWS, 512)],
            [folded.reshape(LAYERS * ROWS * FOLDS, LANES)],
        )
        return own, swap(other)

    def assemble(own, other):
        return jnp.where(
            core == 0, jnp.concatenate([own, other], axis=2), jnp.concatenate([other, own], axis=2)
        )

    shown = spread(height, 1.0 / HALF, "blueprint")
    height, shown = lax.optimization_barrier((height, shown))
    printed = jnp.zeros((LAYERS, ROWS, *block), jnp.float32)
    received = []
    for turn in range(chips):
        operands = [*received, height, height_up, height_down, printed]
        printed, *top = call(
            functools.partial(chain_kernel, turn, tiles),
            "chain",
            [(LAYERS, ROWS, *block), (ROWS, 640)][: 2 if turn < chips - 1 else 1],
            operands,
            scratch=[(48 * FOLDS, LANES)] * 2,
            aliases={len(operands) - 1: 0},
        )
        if turn < chips - 1:
            received = [
                lax.ppermute(
                    top[0],
                    AXES,
                    [
                        (at(2 * turn + c, t), at(2 * turn + 2 + c, t + away))
                        for c in range(2)
                        for t in range(tiles)
                        if 0 <= t + away < tiles
                    ],
                )
                for away in (0, 1, -1)
            ]
        if turn == 0:
            printed, blueprint = lax.optimization_barrier((printed, assemble(*shown)))
    return blueprint, assemble(*spread(printed, 0.5 / HALF, "printed"))


def solution(mesh):
    spec = P("gz", "xy", None)
    return jax.shard_map(local, mesh=mesh, in_specs=(spec,), out_specs=(spec, spec), check_vma=False)
```

```python
import functools
import math

import jax
import jax.numpy as jnp
from jax import lax
from jax.experimental import pallas as pl
from jax.experimental.pallas import tpu as pltpu
from jax.sharding import PartitionSpec as P

LAYERS = 16
ROWS = 16
FOLDS = 8
LANES = 128
STRIDE = 80
HALO = 24
REACH = 3
PART = 768
AXES = ("gz", "xy")

FILTER_R2 = 4.0
PROJ_BETA = 8.0
PROJ_ETA = 0.5
SHARPNESS = 16.0
SMOOTH_EPS = 0.0001
HALF = 0.5 * SHARPNESS / math.log(2.0)
OUTSIDE = -50.0
TINY = 2.0**-100
MARGIN_AT = [sum(15 - j for j in range(k)) for k in range(16)]
MARGIN = MARGIN_AT[15]
SIDE = 20 + 18 + 16


def place():
    slab = lax.axis_index("gz")
    return lax.div(slab, 2), lax.rem(slab, 2), lax.axis_index("xy")


def lane_of(shape=(FOLDS, LANES)):
    return lax.broadcasted_iota(jnp.int32, shape, len(shape) - 1)


def column_mask(core):
    fold = lax.broadcasted_iota(jnp.int32, (FOLDS, LANES), 0)
    column = 384 * core + STRIDE * fold + lane_of() - HALO
    return (column >= 0) & (column < 1024)


def fetch_kernel(design, own, near, far, *refs):
    unused, core, unused = place()
    here = pl.ds(pl.multiple_of(256 * core, LANES), PART)
    there = pl.ds(pl.multiple_of(256 * (1 - core), LANES), PART)
    rim = pl.ds((8 - REACH) * core, REACH)
    *parts, done = refs
    copies = [
        pltpu.make_async_copy(design.at[rim, :, here], far, done.at[0]),
        pltpu.make_async_copy(design.at[rim, :, there], near, done.at[1]),
        pltpu.make_async_copy(design.at[:, :, here], own, done.at[2]),
    ]
    for i, part in enumerate(parts):
        side = pl.ds(pl.multiple_of(256 * (1 - core) + 256 * i, LANES), 256)
        copies.append(pltpu.make_async_copy(design.at[:, :, side], part, done.at[3 + i]))
    for copy in copies:
        copy.start()
    for copy in copies:
        copy.wait()


def fold_rows(tiles, lane, store):
    for s in range(FOLDS):
        a, shift = divmod(LANES - HALO + STRIDE * s, LANES)
        block = tiles[a]
        if shift:
            first = pltpu.roll(tiles[a], LANES - shift, 1)
            second = pltpu.roll(tiles[a + 1], LANES - shift, 1)
            block = jnp.where(lane < LANES - shift, first, second)
        store(s, block)


def unfold_rows(blocks, lane):
    tiles = []
    for a in range(5):
        tile = None
        for s in range(FOLDS):
            low = max(LANES * a, STRIDE * s)
            if low >= min(LANES * a + LANES, STRIDE * s + STRIDE):
                continue
            piece = pltpu.roll(blocks[s], (STRIDE * s - LANES * a - HALO) % LANES, 1)
            tile = piece if tile is None else jnp.where(lane >= low - LANES * a, piece, tile)
        tiles.append(tile)
    return tiles


def fold_kernel(own, near, far, first, second, third, out, to_down, to_up):
    unused, core, unused = place()
    lane = lane_of()

    def fold(source, base, count):
        def layer(i, carry):
            for group in range(2):
                tiles = []
                for a in range(7):
                    if isinstance(source, tuple):
                        sides = [
                            source[b // 2][i, pl.ds(8 * group, 8), pl.ds(b % 2 * LANES, LANES)]
                            for b in (max(a - 1, 0), min(a, 5))
                        ]
                        tile = jnp.where(core == 0, *sides)
                    else:
                        at = jnp.clip(a - 1 + core, 0, 5) * LANES
                        tile = source[i, pl.ds(8 * group, 8), pl.ds(pl.multiple_of(at, LANES), LANES)]
                    if a == 0:
                        tile = jnp.where(core == 0, 0.0, tile)
                    if a == 6:
                        tile = jnp.where(core == 1, 0.0, tile)
                    tiles.append(tile)
                row = ((base + i) * ROWS + 8 * group) * FOLDS

                def store(s, block):
                    out[pl.ds(row + s, 8, stride=FOLDS), :] = block

                fold_rows(tiles, lane, store)
            return carry

        lax.fori_loop(0, count, layer, 0, unroll=count)

    fold(own, REACH + 8 * core, 8)
    fold((first, second, third), REACH + 8 * (1 - core), 8)
    fold(near, 19 * core, REACH)
    fold(far, 19 * (1 - core), REACH)
    at = 0
    for away in range(REACH):
        for i in range(1 + away, 21 - away):
            to_down[at] = out[pl.ds((i * ROWS + 15 - away) * FOLDS, FOLDS), :]
            to_up[at] = out[pl.ds((i * ROWS + away) * FOLDS, FOLDS), :]
            at += 1


def filter_kernel(count_chips, count_tiles, own, up, down, height, to_down, to_up, cells, first, second, packed):
    chip, core, tile = place()
    inside = column_mask(core)
    scale = jnp.where(inside, 1.0 / (1.0 + 6.0 * FILTER_R2), 0.0)
    above = jnp.where(tile > 0, 1.0, 0.0)
    below = jnp.where(tile < count_tiles - 1, 1.0, 0.0)

    def gather(i, carry):
        cells[i, pl.ds(REACH, ROWS)] = own[i]
        return carry

    lax.fori_loop(0, 22, gather, 0, unroll=22)
    at = 0
    for away in range(REACH):
        for i in range(1 + away, 21 - away):
            cells[i, REACH - 1 - away] = up[at]
            cells[i, REACH + ROWS + away] = down[at]
            at += 1

    def sweep(source, step, store):
        rim = REACH - step

        def layer(i, rows):
            held = jnp.where(((chip == 0) & (i < REACH)) | ((chip == count_chips - 1) & (i >= REACH + LAYERS)), 0.0, scale)
            for r in rows:
                middle = source[i, r]
                total = source[i - 1, r] + source[i + 1, r] + source[i, r - 1] + source[i, r + 1]
                total = total + pltpu.roll(middle, 1, 1) + pltpu.roll(middle, LANES - 1, 1)
                factor = held
                if r < REACH:
                    factor = held * above
                if r >= REACH + ROWS:
                    factor = held * below
                store(i, r, (cells[i, r] + FILTER_R2 * total) * factor)

        def body(i, carry):
            layer(i, range(REACH - rim, REACH + ROWS + rim))
            return carry

        for away in range(rim):
            for i in (REACH - rim + away, REACH + LAYERS + rim - 1 - away):
                layer(i, range(REACH - away, REACH + ROWS + away))
        lax.fori_loop(REACH, REACH + LAYERS, body, 0, unroll=LAYERS)

    def keep(target):
        def store(i, r, value):
            target[i, r] = value

        return store

    base = math.tanh(PROJ_BETA * PROJ_ETA)
    gain = HALF / (math.tanh(PROJ_BETA * PROJ_ETA) + math.tanh(PROJ_BETA * (1.0 - PROJ_ETA)))

    def project(i, r, field):
        value = gain * (base + jnp.tanh(PROJ_BETA * field - PROJ_BETA * PROJ_ETA))
        height[i - REACH, r - REACH] = jnp.where(inside, value, OUTSIDE)

    sweep(cells, 1, keep(first))
    sweep(first, 2, keep(second))
    sweep(second, 3, project)
    lane = lane_of()
    for target, low in ((to_down, 1), (to_up, 0)):
        for k in range(15):
            rows = height[k, pl.ds(low * (k + 1), 15 - k)]
            packed[pl.ds(MARGIN_AT[k] * FOLDS, (15 - k) * FOLDS), :] = rows.reshape((15 - k) * FOLDS, LANES)
        for group in range(MARGIN // 8):
            blocks = [packed[pl.ds(8 * group * FOLDS + s, 8, stride=FOLDS), :] for s in range(FOLDS)]
            for a, tile in enumerate(unfold_rows(blocks, lane)):
                target[pl.ds(8 * group, 8), pl.ds(LANES * a, LANES)] = tile


def widen_kernel(edge, rows, out):
    unused, core, tile = place()
    lane = lane_of()
    zero = jnp.zeros((8, LANES), jnp.float32)
    for group in range(MARGIN // 8):
        tiles = [rows[pl.ds(8 * group, 8), pl.ds(LANES * a, LANES)] for a in range(5)]

        def store(s, block):
            out[pl.ds(8 * group * FOLDS + s, 8, stride=FOLDS), :] = block

        fold_rows([zero, *tiles, zero], lane, store)
    inside = column_mask(core) & (tile != edge)
    for r in range(MARGIN):
        at = pl.ds(r * FOLDS, FOLDS)
        out[at, :] = jnp.where(inside, out[at, :], OUTSIDE)


def chain_kernel(turn, count_tiles, *refs):
    received, refs = (refs[:3], refs[3:]) if turn else ((), refs)
    height, height_up, height_down, unused, printed, *top, even, odd = refs
    chip, core, tile = place()

    def row(j):
        return pl.ds(j * FOLDS, FOLDS)

    @pl.when(chip == turn)
    def run():
        inside = column_mask(core)
        lane = lane_of()
        if turn:
            middle, up, down = received
            zero = jnp.zeros((8, LANES), jnp.float32)
            for source, first in ((up, 0), (middle, ROWS), (down, 2 * ROWS)):
                for group in range(2):
                    tiles = [source[pl.ds(8 * group, 8), pl.ds(LANES * a, LANES)] for a in range(5)]

                    def store(s, block):
                        even[pl.ds((first + 8 * group) * FOLDS + s, 8, stride=FOLDS), :] = block + TINY

                    fold_rows([zero, *tiles, zero], lane, store)
        else:
            ones = jnp.where(inside, math.exp(SHARPNESS), TINY)
            ones_up = jnp.where(tile > 0, ones, TINY)
            ones_down = jnp.where(tile < count_tiles - 1, ones, TINY)
            for r in range(ROWS):
                even[row(r), :] = ones_up
                even[row(ROWS + r), :] = ones
                even[row(2 * ROWS + r), :] = ones_down
        level = HALF * math.sqrt(SMOOTH_EPS)
        for k in range(LAYERS):
            source, target = (even, odd) if k % 2 == 0 else (odd, even)
            for j in range(k + 1, 47 - k):
                total = source[row(j - 1), :] + source[row(j), :] + source[row(j + 1), :]
                total = total + pltpu.roll(total, 1, 1) + pltpu.roll(total, LANES - 1, 1)
                support = jnp.log(total) * (0.5 / math.log(2.0)) - 0.5 * math.log2(9.0)
                if j < ROWS:
                    blue = height_up[MARGIN_AT[k] + j - 1 - k]
                elif j < 2 * ROWS:
                    blue = height[k, j - ROWS]
                else:
                    blue = height_down[MARGIN_AT[k] + j - 2 * ROWS]
                gap = blue - support
                square = gap * gap + level * level
                value = (blue + support + level) - square * lax.rsqrt(square)
                weight = jnp.exp2(value)
                if ROWS <= j < 2 * ROWS:
                    printed[k, j - ROWS] = value
                if k < LAYERS - 1 or top:
                    target[row(j), :] = weight
        for group in range(2 if top else 0):
            first = (ROWS + 8 * group) * FOLDS
            blocks = [even[pl.ds(first + s, 8, stride=FOLDS), :] for s in range(FOLDS)]
            for a, piece in enumerate(unfold_rows(blocks, lane)):
                top[0][pl.ds(8 * group, 8), pl.ds(LANES * a, LANES)] = piece


def unfold_kernel(scale, folded, own, partner):
    unused, core, unused = place()
    lane = lane_of()

    def unfold(target, base):
        def layer(i, carry):
            for group in range(2):
                row = ((base + i) * ROWS + 8 * group) * FOLDS
                blocks = [folded[pl.ds(row + s, 8, stride=FOLDS), :] * scale for s in range(FOLDS)]
                tiles = unfold_rows(blocks, lane)
                for a in range(4):
                    target[i, pl.ds(8 * group, 8), pl.ds(LANES * a, LANES)] = jnp.where(core == 0, tiles[a], tiles[a + 1])
            return carry

        lax.fori_loop(0, 8, layer, 0, unroll=8)

    unfold(own, 8 * core)
    unfold(partner, 8 * (1 - core))


def call(kernel, name, outs, operands, scratch=(), aliases=None):
    held = [pltpu.with_memory_space_constraint(x, pltpu.VMEM) for x in operands]
    vmem = pl.BlockSpec(memory_space=pltpu.VMEM)
    return pl.pallas_call(
        kernel,
        name=name,
        out_shape=[pltpu.VMEM(shape, jnp.float32) for shape in outs],
        in_specs=[vmem] * len(held),
        out_specs=[vmem] * len(outs),
        scratch_shapes=[pltpu.VMEM(shape, jnp.float32) for shape in scratch],
        input_output_aliases=aliases or {},
        compiler_params=pltpu.CompilerParams(vmem_limit_bytes=24 * 1024 * 1024),
    )(*held)


def local(design):
    slabs = lax.axis_size("gz")
    tiles = lax.axis_size("xy")
    chips = slabs // 2
    unused, core, unused = place()

    def at(slab, tile):
        return slab * tiles + tile

    def swap(block):
        return lax.ppermute(block, "gz", [(i, i ^ 1) for i in range(slabs)])

    def from_up(block):
        return lax.ppermute(block, "xy", [(i, i + 1) for i in range(tiles - 1)])

    def from_down(block):
        return lax.ppermute(block, "xy", [(i + 1, i) for i in range(tiles - 1)])

    crossing = [(i, j) for k in range(1, chips) for i, j in ((2 * k - 1, 2 * k), (2 * k, 2 * k - 1))]
    straight = [(i, j) for k in range(1, chips) for i, j in ((2 * k - 1, 2 * k + 1), (2 * k, 2 * k - 2))]
    vmem = pl.BlockSpec(memory_space=pltpu.VMEM)
    whole, rim = (8, ROWS, PART), (REACH, ROWS, PART)
    part = (8, ROWS, 256)
    own, near, far, *parts = pl.pallas_call(
        fetch_kernel,
        name="fetch",
        out_shape=[pltpu.VMEM(shape, jnp.float32) for shape in (whole, rim, rim, part, part, part)],
        in_specs=[pl.BlockSpec(memory_space=pltpu.HBM)],
        out_specs=[vmem] * 6,
        scratch_shapes=[pltpu.SemaphoreType.DMA((6,))],
    )(pltpu.with_memory_space_constraint(design, pltpu.HBM))
    far = lax.ppermute(far, "gz", straight)
    near = lax.ppermute(near, "gz", crossing)
    parts = [swap(part) for part in parts]
    block = (FOLDS, LANES)
    folded, to_down, to_up = call(
        fold_kernel,
        "fold",
        [(22 * ROWS * FOLDS, LANES), (SIDE, *block), (SIDE, *block)],
        [own, near, far, *parts],
    )
    height, to_down, to_up = call(
        functools.partial(filter_kernel, chips, tiles),
        "filter",
        [(LAYERS, ROWS, *block), (MARGIN, 640), (MARGIN, 640)],
        [folded.reshape(22, ROWS, *block), from_up(to_down), from_down(to_up)],
        scratch=[(22, ROWS + 2 * REACH, *block)] * 3 + [(MARGIN * FOLDS, LANES)],
    )

    def widen(rows, edge, name):
        (out,) = call(functools.partial(widen_kernel, edge), name, [(MARGIN * FOLDS, LANES)], [rows])
        return out.reshape(MARGIN, *block)

    height_up = widen(from_up(to_down), 0, "widen_up")
    height_down = widen(from_down(to_up), tiles - 1, "widen_down")

    def spread(folded, scale, name):
        own, other = call(
            functools.partial(unfold_kernel, scale),
            name,
            [(8, ROWS, 512), (8, ROWS, 512)],
            [folded.reshape(LAYERS * ROWS * FOLDS, LANES)],
        )
        return own, swap(other)

    def assemble(own, other):
        return jnp.where(
            core == 0, jnp.concatenate([own, other], axis=2), jnp.concatenate([other, own], axis=2)
        )

    shown = spread(height, 1.0 / HALF, "blueprint")
    height, shown = lax.optimization_barrier((height, shown))
    printed = jnp.zeros((LAYERS, ROWS, *block), jnp.float32)
    received = []
    for turn in range(chips):
        operands = [*received, height, height_up, height_down, printed]
        printed, *top = call(
            functools.partial(chain_kernel, turn, tiles),
            "chain",
            [(LAYERS, ROWS, *block), (ROWS, 640)][: 2 if turn < chips - 1 else 1],
            operands,
            scratch=[(48 * FOLDS, LANES)] * 2,
            aliases={len(operands) - 1: 0},
        )
        if turn < chips - 1:
            received = [
                lax.ppermute(
                    top[0],
                    AXES,
                    [
                        (at(2 * turn + c, t), at(2 * turn + 2 + c, t + away))
                        for c in range(2)
                        for t in range(tiles)
                        if 0 <= t + away < tiles
                    ],
                )
                for away in (0, 1, -1)
            ]
        if turn == 0:
            printed, blueprint = lax.optimization_barrier((printed, assemble(*shown)))
    return blueprint, assemble(*spread(printed, 0.5 / HALF, "printed"))


def solution(mesh):
    spec = P("gz", "xy", None)
    return jax.shard_map(local, mesh=mesh, in_specs=(spec,), out_specs=(spec, spec), check_vma=False)
```

```python
import functools
import math

import jax
import jax.numpy as jnp
from jax import lax
from jax.experimental import pallas as pl
from jax.experimental.pallas import tpu as pltpu
from jax.sharding import PartitionSpec as P

LAYERS = 16
ROWS = 16
FOLDS = 8
LANES = 128
STRIDE = 80
HALO = 24
REACH = 3
PART = 768
AXES = ("gz", "xy")

FILTER_R2 = 4.0
PROJ_BETA = 8.0
PROJ_ETA = 0.5
SHARPNESS = 16.0
SMOOTH_EPS = 0.0001
HALF = 0.5 * SHARPNESS / math.log(2.0)
OUTSIDE = -50.0
TINY = 2.0**-100
MARGIN_AT = [sum(15 - j for j in range(k)) for k in range(16)]
MARGIN = MARGIN_AT[15]
SIDE = 20 + 18 + 16


def place():
    slab = lax.axis_index("gz")
    return lax.div(slab, 2), lax.rem(slab, 2), lax.axis_index("xy")


def window_of(chip, core):
    return lax.rem(chip + core, 2)


def lane_of(shape=(FOLDS, LANES)):
    return lax.broadcasted_iota(jnp.int32, shape, len(shape) - 1)


def column_mask(window):
    fold = lax.broadcasted_iota(jnp.int32, (FOLDS, LANES), 0)
    column = 384 * window + STRIDE * fold + lane_of() - HALO
    return (column >= 0) & (column < 1024)


def fetch_kernel(design, own, partner, near, far, done):
    chip, core, unused = place()
    window = window_of(chip, core)
    here = pl.ds(pl.multiple_of(256 * window, LANES), PART)
    there = pl.ds(pl.multiple_of(256 * (1 - window), LANES), PART)
    rim = pl.ds((8 - REACH) * core, REACH)
    copies = [
        pltpu.make_async_copy(design.at[rim, :, there], far, done.at[0]),
        pltpu.make_async_copy(design.at[rim, :, here], near, done.at[1]),
        pltpu.make_async_copy(design.at[:, :, there], partner, done.at[2]),
        pltpu.make_async_copy(design.at[:, :, here], own, done.at[3]),
    ]
    for copy in copies:
        copy.start()
    for copy in copies:
        copy.wait()


def fold_rows(tiles, lane, store):
    for s in range(FOLDS):
        a, shift = divmod(LANES - HALO + STRIDE * s, LANES)
        block = tiles[a]
        if shift:
            first = pltpu.roll(tiles[a], LANES - shift, 1)
            second = pltpu.roll(tiles[a + 1], LANES - shift, 1)
            block = jnp.where(lane < LANES - shift, first, second)
        store(s, block)


def unfold_rows(blocks, lane):
    tiles = []
    for a in range(5):
        tile = None
        for s in range(FOLDS):
            low = max(LANES * a, STRIDE * s)
            if low >= min(LANES * a + LANES, STRIDE * s + STRIDE):
                continue
            piece = pltpu.roll(blocks[s], (STRIDE * s - LANES * a - HALO) % LANES, 1)
            tile = piece if tile is None else jnp.where(lane >= low - LANES * a, piece, tile)
        tiles.append(tile)
    return tiles


def fold_kernel(own, partner, near, far, out, to_down, to_up):
    chip, core, unused = place()
    window = window_of(chip, core)
    lane = lane_of()

    def fold(source, base, count):
        def layer(i, carry):
            for group in range(2):
                tiles = []
                for a in range(7):
                    at = jnp.clip(a - 1 + window, 0, 5) * LANES
                    tile = source[i, pl.ds(8 * group, 8), pl.ds(pl.multiple_of(at, LANES), LANES)]
                    if a == 0:
                        tile = jnp.where(window == 0, 0.0, tile)
                    if a == 6:
                        tile = jnp.where(window == 1, 0.0, tile)
                    tiles.append(tile)
                row = ((base + i) * ROWS + 8 * group) * FOLDS

                def store(s, block):
                    out[pl.ds(row + s, 8, stride=FOLDS), :] = block

                fold_rows(tiles, lane, store)
            return carry

        lax.fori_loop(0, count, layer, 0, unroll=count)

    fold(own, REACH + 8 * core, 8)
    fold(partner, REACH + 8 * (1 - core), 8)
    fold(near, 19 * core, REACH)
    fold(far, 19 * (1 - core), REACH)
    at = 0
    for away in range(REACH):
        for i in range(1 + away, 21 - away):
            to_down[at] = out[pl.ds((i * ROWS + 15 - away) * FOLDS, FOLDS), :]
            to_up[at] = out[pl.ds((i * ROWS + away) * FOLDS, FOLDS), :]
            at += 1


def filter_kernel(count_chips, count_tiles, own, up, down, height, to_down, to_up, cells, first, second, packed):
    chip, core, tile = place()
    inside = column_mask(window_of(chip, core))
    scale = jnp.where(inside, 1.0 / (1.0 + 6.0 * FILTER_R2), 0.0)
    above = jnp.where(tile > 0, 1.0, 0.0)
    below = jnp.where(tile < count_tiles - 1, 1.0, 0.0)

    def gather(i, carry):
        cells[i, pl.ds(REACH, ROWS)] = own[i]
        return carry

    lax.fori_loop(0, 22, gather, 0, unroll=22)
    at = 0
    for away in range(REACH):
        for i in range(1 + away, 21 - away):
            cells[i, REACH - 1 - away] = up[at]
            cells[i, REACH + ROWS + away] = down[at]
            at += 1

    def sweep(source, step, store):
        rim = REACH - step

        def layer(i, rows):
            held = jnp.where(((chip == 0) & (i < REACH)) | ((chip == count_chips - 1) & (i >= REACH + LAYERS)), 0.0, scale)
            for r in rows:
                middle = source[i, r]
                total = source[i - 1, r] + source[i + 1, r] + source[i, r - 1] + source[i, r + 1]
                total = total + pltpu.roll(middle, 1, 1) + pltpu.roll(middle, LANES - 1, 1)
                factor = held
                if r < REACH:
                    factor = held * above
                if r >= REACH + ROWS:
                    factor = held * below
                store(i, r, (cells[i, r] + FILTER_R2 * total) * factor)

        def body(i, carry):
            layer(i, range(REACH - rim, REACH + ROWS + rim))
            return carry

        for away in range(rim):
            for i in (REACH - rim + away, REACH + LAYERS + rim - 1 - away):
                layer(i, range(REACH - away, REACH + ROWS + away))
        lax.fori_loop(REACH, REACH + LAYERS, body, 0, unroll=LAYERS)

    def keep(target):
        def store(i, r, value):
            target[i, r] = value

        return store

    base = math.tanh(PROJ_BETA * PROJ_ETA)
    gain = HALF / (math.tanh(PROJ_BETA * PROJ_ETA) + math.tanh(PROJ_BETA * (1.0 - PROJ_ETA)))

    def project(i, r, field):
        value = gain * (base + jnp.tanh(PROJ_BETA * field - PROJ_BETA * PROJ_ETA))
        height[i - REACH, r - REACH] = jnp.where(inside, value, OUTSIDE)

    sweep(cells, 1, keep(first))
    sweep(first, 2, keep(second))
    sweep(second, 3, project)
    lane = lane_of()
    for target, low in ((to_down, 1), (to_up, 0)):
        for k in range(15):
            rows = height[k, pl.ds(low * (k + 1), 15 - k)]
            packed[pl.ds(MARGIN_AT[k] * FOLDS, (15 - k) * FOLDS), :] = rows.reshape((15 - k) * FOLDS, LANES)
        for group in range(MARGIN // 8):
            blocks = [packed[pl.ds(8 * group * FOLDS + s, 8, stride=FOLDS), :] for s in range(FOLDS)]
            for a, tile in enumerate(unfold_rows(blocks, lane)):
                target[pl.ds(8 * group, 8), pl.ds(LANES * a, LANES)] = tile


def widen_kernel(edge, rows, out):
    chip, core, tile = place()
    lane = lane_of()
    zero = jnp.zeros((8, LANES), jnp.float32)
    for group in range(MARGIN // 8):
        tiles = [rows[pl.ds(8 * group, 8), pl.ds(LANES * a, LANES)] for a in range(5)]

        def store(s, block):
            out[pl.ds(8 * group * FOLDS + s, 8, stride=FOLDS), :] = block

        fold_rows([zero, *tiles, zero], lane, store)
    inside = column_mask(window_of(chip, core)) & (tile != edge)
    for r in range(MARGIN):
        at = pl.ds(r * FOLDS, FOLDS)
        out[at, :] = jnp.where(inside, out[at, :], OUTSIDE)


def chain_kernel(turn, count_tiles, *refs):
    received, refs = (refs[:3], refs[3:]) if turn else ((), refs)
    height, height_up, height_down, unused, printed, *top, even, odd = refs
    chip, core, tile = place()

    def row(j):
        return pl.ds(j * FOLDS, FOLDS)

    @pl.when(chip == turn)
    def run():
        inside = column_mask(window_of(chip, core))
        lane = lane_of()
        if turn:
            middle, up, down = received
            zero = jnp.zeros((8, LANES), jnp.float32)
            for source, first in ((up, 0), (middle, ROWS), (down, 2 * ROWS)):
                for group in range(2):
                    tiles = [source[pl.ds(8 * group, 8), pl.ds(LANES * a, LANES)] for a in range(5)]

                    def store(s, block):
                        even[pl.ds((first + 8 * group) * FOLDS + s, 8, stride=FOLDS), :] = block + TINY

                    fold_rows([zero, *tiles, zero], lane, store)
        else:
            ones = jnp.where(inside, math.exp(SHARPNESS), TINY)
            ones_up = jnp.where(tile > 0, ones, TINY)
            ones_down = jnp.where(tile < count_tiles - 1, ones, TINY)
            for r in range(ROWS):
                even[row(r), :] = ones_up
                even[row(ROWS + r), :] = ones
                even[row(2 * ROWS + r), :] = ones_down
        level = HALF * math.sqrt(SMOOTH_EPS)
        for k in range(LAYERS):
            source, target = (even, odd) if k % 2 == 0 else (odd, even)
            for j in range(k + 1, 47 - k):
                total = source[row(j - 1), :] + source[row(j), :] + source[row(j + 1), :]
                total = total + pltpu.roll(total, 1, 1) + pltpu.roll(total, LANES - 1, 1)
                support = jnp.log(total) * (0.5 / math.log(2.0)) - 0.5 * math.log2(9.0)
                if j < ROWS:
                    blue = height_up[MARGIN_AT[k] + j - 1 - k]
                elif j < 2 * ROWS:
                    blue = height[k, j - ROWS]
                else:
                    blue = height_down[MARGIN_AT[k] + j - 2 * ROWS]
                gap = blue - support
                square = gap * gap + level * level
                value = (blue + support + level) - square * lax.rsqrt(square)
                weight = jnp.exp2(value)
                if ROWS <= j < 2 * ROWS:
                    printed[k, j - ROWS] = value
                if k < LAYERS - 1 or top:
                    target[row(j), :] = weight
        for group in range(2 if top else 0):
            first = (ROWS + 8 * group) * FOLDS
            blocks = [even[pl.ds(first + s, 8, stride=FOLDS), :] for s in range(FOLDS)]
            for a, piece in enumerate(unfold_rows(blocks, lane)):
                top[0][pl.ds(8 * group, 8), pl.ds(LANES * a, LANES)] = piece


def unfold_kernel(scale, folded, own, partner):
    chip, core, unused = place()
    window = window_of(chip, core)
    lane = lane_of()

    def unfold(target, base):
        def layer(i, carry):
            for group in range(2):
                row = ((base + i) * ROWS + 8 * group) * FOLDS
                blocks = [folded[pl.ds(row + s, 8, stride=FOLDS), :] * scale for s in range(FOLDS)]
                tiles = unfold_rows(blocks, lane)
                for a in range(4):
                    target[i, pl.ds(8 * group, 8), pl.ds(LANES * a, LANES)] = jnp.where(window == 0, tiles[a], tiles[a + 1])
            return carry

        lax.fori_loop(0, 8, layer, 0, unroll=8)

    unfold(own, 8 * core)
    unfold(partner, 8 * (1 - core))


def call(kernel, name, outs, operands, scratch=(), aliases=None):
    held = [pltpu.with_memory_space_constraint(x, pltpu.VMEM) for x in operands]
    vmem = pl.BlockSpec(memory_space=pltpu.VMEM)
    return pl.pallas_call(
        kernel,
        name=name,
        out_shape=[pltpu.VMEM(shape, jnp.float32) for shape in outs],
        in_specs=[vmem] * len(held),
        out_specs=[vmem] * len(outs),
        scratch_shapes=[pltpu.VMEM(shape, jnp.float32) for shape in scratch],
        input_output_aliases=aliases or {},
        compiler_params=pltpu.CompilerParams(vmem_limit_bytes=24 * 1024 * 1024),
    )(*held)


def local(design):
    slabs = lax.axis_size("gz")
    tiles = lax.axis_size("xy")
    chips = slabs // 2
    chip, core, unused = place()
    window = window_of(chip, core)

    def at(slab, tile):
        return slab * tiles + tile

    def swap(block):
        return lax.ppermute(block, "gz", [(i, i ^ 1) for i in range(slabs)])

    def from_up(block):
        return lax.ppermute(block, "xy", [(i, i + 1) for i in range(tiles - 1)])

    def from_down(block):
        return lax.ppermute(block, "xy", [(i + 1, i) for i in range(tiles - 1)])

    crossing = [(i, j) for k in range(1, chips) for i, j in ((2 * k - 1, 2 * k), (2 * k, 2 * k - 1))]
    straight = [(i, j) for k in range(1, chips) for i, j in ((2 * k - 1, 2 * k + 1), (2 * k, 2 * k - 2))]
    vmem = pl.BlockSpec(memory_space=pltpu.VMEM)
    whole, rim = (8, ROWS, PART), (REACH, ROWS, PART)
    own, partner, near, far = pl.pallas_call(
        fetch_kernel,
        name="fetch",
        out_shape=[pltpu.VMEM(shape, jnp.float32) for shape in (whole, whole, rim, rim)],
        in_specs=[pl.BlockSpec(memory_space=pltpu.HBM)],
        out_specs=[vmem] * 4,
        scratch_shapes=[pltpu.SemaphoreType.DMA((4,))],
    )(pltpu.with_memory_space_constraint(design, pltpu.HBM))
    far = lax.ppermute(far, "gz", straight)
    near = lax.ppermute(near, "gz", crossing)
    partner = swap(partner)
    block = (FOLDS, LANES)
    folded, to_down, to_up = call(
        fold_kernel,
        "fold",
        [(22 * ROWS * FOLDS, LANES), (SIDE, *block), (SIDE, *block)],
        [own, partner, near, far],
    )
    height, to_down, to_up = call(
        functools.partial(filter_kernel, chips, tiles),
        "filter",
        [(LAYERS, ROWS, *block), (MARGIN, 640), (MARGIN, 640)],
        [folded.reshape(22, ROWS, *block), from_up(to_down), from_down(to_up)],
        scratch=[(22, ROWS + 2 * REACH, *block)] * 3 + [(MARGIN * FOLDS, LANES)],
    )

    def widen(rows, edge, name):
        (out,) = call(functools.partial(widen_kernel, edge), name, [(MARGIN * FOLDS, LANES)], [rows])
        return out.reshape(MARGIN, *block)

    height_up = widen(from_up(to_down), 0, "widen_up")
    height_down = widen(from_down(to_up), tiles - 1, "widen_down")

    def spread(folded, scale, name):
        own, other = call(
            functools.partial(unfold_kernel, scale),
            name,
            [(8, ROWS, 512), (8, ROWS, 512)],
            [folded.reshape(LAYERS * ROWS * FOLDS, LANES)],
        )
        return own, swap(other)

    def assemble(own, other):
        return jnp.where(
            window == 0, jnp.concatenate([own, other], axis=2), jnp.concatenate([other, own], axis=2)
        )

    shown = spread(height, 1.0 / HALF, "blueprint")
    height, shown = lax.optimization_barrier((height, shown))
    printed = jnp.zeros((LAYERS, ROWS, *block), jnp.float32)
    received = []
    for turn in range(chips):
        operands = [*received, height, height_up, height_down, printed]
        printed, *top = call(
            functools.partial(chain_kernel, turn, tiles),
            "chain",
            [(LAYERS, ROWS, *block), (ROWS, 640)][: 2 if turn < chips - 1 else 1],
            operands,
            scratch=[(48 * FOLDS, LANES)] * 2,
            aliases={len(operands) - 1: 0},
        )
        if turn < chips - 1:
            received = [
                lax.ppermute(
                    top[0],
                    AXES,
                    [
                        (at(2 * turn + c, t), at(2 * turn + 3 - c, t + away))
                        for c in range(2)
                        for t in range(tiles)
                        if 0 <= t + away < tiles
                    ],
                )
                for away in (0, 1, -1)
            ]
        if turn == 0:
            printed, blueprint = lax.optimization_barrier((printed, assemble(*shown)))
    return blueprint, assemble(*spread(printed, 0.5 / HALF, "printed"))


def solution(mesh):
    spec = P("gz", "xy", None)
    return jax.shard_map(local, mesh=mesh, in_specs=(spec,), out_specs=(spec, spec), check_vma=False)
```
